128 devices in a mesh: rep: 4 (over y), dev: 32 (over x, z, core).
Axes of the slice: x: 4, y: 4, z: 4, core: 2. Of those that a mesh axis runs over, the one named last changes fastest.
Arguments:
- queries: bfloat16 [256, 128, 576], P(('rep', 'dev')), parts along dimension 0, may hold values from -250 to 250
- latent_cache: bfloat16 [256, 1024, 576], P(('rep', 'dev')), parts along dimension 0, may hold values from -10 to 10
- lengths: int32 [256], P('rep'), parts along dimension 0, may hold values from 1 to 1024, 32768 in all
- trade_slot: int32 [64], P('rep'), parts along dimension 0, may hold values from 0 to 1
- tokens: bfloat16 [256, 3584], P(('rep', 'dev')), parts along dimension 0, may hold values from -6 to 6
- routing: int32 [256, 8], P(('rep', 'dev')), parts along dimension 0, may hold values from 0 to 31, all different within a row; in each aligned block of 2 rows (0 to 1, 2 to 3, ...) at most 2 rows name the same one
- gate_weights: float32 [256, 8], P(('rep', 'dev')), parts along dimension 0, may hold values from 0.05 to 0.5
- w_gate: bfloat16 [32, 3584, 1024], P('dev'), may hold values from -0.09375 to 0.09375
- w_up: bfloat16 [32, 3584, 1024], P('dev'), may hold values from -0.09375 to 0.09375
- w_down: bfloat16 [32, 1024, 3584], P('dev'), may hold values from -0.1875 to 0.1875
Outputs:
- attended: bfloat16 [256, 128, 512], P(('rep', 'dev')), parts along dimension 0
- expert_out: bfloat16 [256, 3584], P(('rep', 'dev')), parts along dimension 0
The draws below stay inside these ranges and needn't reach their ends.
There are 4 independent parts, one for each index of `rep`. The reference program is written for one: setup_inputs(seed, part) draws one part's arguments, and reference() takes and returns one part's arrays. A program takes and returns all parts, laid end to end along the dimension named above; an argument that names none is the same for every part. Nothing has to cross between parts.
Inputs may be any that keep to these rules, and one draw needn't show every extreme that they name: `routing`: each token names 8 different experts; among the tokens of one device no expert is named more than 2 times.
All inputs are finite; a program needn't handle non-finite values.
Results may differ from the reference program's by a relative error of at most 0.011.
Values may be sent and summed in bfloat16 or wider, within the bound.
A program may use at most 128 MiB of HBM per device.

```python
import math
import jax
import jax.numpy as jnp
import numpy as np
from jax import lax

D = 3584
FF = 1024
HEADS = 128
LAT = 512
ROPE = 64
TOP = 8
REQ_DEV = 2
CTX = 1024
TOK_DEV = 2
EXPERTS = 32
CAP = 2
REQUESTS = 64
TOKENS = 64
PAIRS = 16
N_DEV = 32


def latent_rows(key):
    base = jnp.clip(jax.random.normal(key, (REQUESTS, CTX, LAT + ROPE), jnp.float32), -4.0, 4.0)
    column = jnp.arange(LAT + ROPE)[None, None, :]
    base = jnp.where(column < LAT, base, base)
    second = (jnp.arange(CTX)[None, :, None] == 1) & (column >= LAT)
    return jnp.where(second, base, base)


def draw_latent_cache(key, part):
    values = latent_rows(key)
    return values.astype(jnp.bfloat16)


def draw_queries(key, part):
    key = jax.random.fold_in(key, 7)
    values = 0.5 * jnp.clip(jax.random.normal(key, (REQUESTS, HEADS, LAT + ROPE), jnp.float32), -4.0, 4.0)
    return values.astype(jnp.bfloat16)


def place_ends(values, key, low, top_value):
    spot = [jax.random.randint(jax.random.fold_in(key, axis), (), 0, length) for axis, length in enumerate(values.shape)]
    widest = values.shape.index(max(values.shape))
    beside = spot[:widest] + [(spot[widest] + 1) % values.shape[widest]] + spot[widest + 1:]
    return values.at[tuple(spot)].set(low).at[tuple(beside)].set(top_value)


def shard_levels(key, shape, split, least, high):
    factor_of = 1.0
    for dim, blocks in split:
        steps = jax.random.uniform(jax.random.fold_in(jax.random.fold_in(key, 6), dim), (blocks,), jnp.float32, least / len(split), high / len(split))
        factor_of = factor_of * jnp.repeat(jnp.exp(steps), shape[dim] // blocks).reshape((-1,) + (1,) * (len(shape) - 1 - dim))
    return factor_of


def length_profile(amount, total, most, lean):
    weights = [(1 << 20) // math.isqrt(standing ** lean) + 1 for standing in range(2, amount + 1)]
    surplus, holding = total - most - (amount - 1), [1] * (amount - 1)
    while surplus > 0:
        candidates = [i for i in range(amount - 1) if holding[i] < most]
        mass, left = sum([weights[i] for i in candidates]), surplus
        for i in candidates:
            more = min(most - holding[i], max(1, left * weights[i] // mass), surplus)
            holding[i] = holding[i] + more
            surplus = surplus - more
    return np.array([most] + holding)


def uneven(rng, amount, total, reach, slope):
    if amount == 2:
        one = jax.random.randint(rng, (), max(1, total - reach), min(reach, total - 1) + 1)
        return jnp.stack([one, total - one])
    sizes = jnp.asarray(length_profile(amount, total, reach, slope), jnp.int32)
    pairs = (amount - 1) // 2
    giver, receiver = sizes[1:1 + 2 * pairs:2], sizes[2:2 + 2 * pairs:2]
    margin = jnp.minimum(giver - 1, reach - receiver)
    moved = jax.random.randint(jax.random.fold_in(rng, 1), (pairs,), 0, 1 << 20) % (margin + 1)
    sizes = sizes.at[1:1 + 2 * pairs:2].set(giver - moved).at[2:2 + 2 * pairs:2].set(receiver + moved)
    return sizes[jax.random.permutation(jax.random.fold_in(rng, 2), amount)]


def assign_block(rng, own, number, rows, number_of, top, most, skew):
    ranking = jax.random.permutation(rng, number_of)
    packed, usual = portions_of(number_of, rows * top, most, skew, True), portions_of(number_of, rows * top, most, skew, False)
    places = jnp.arange(number_of)

    def named(tallies, turn):
        used = int((tallies > 0).sum())
        fixed = max(1, used // 4)
        passed = fixed + (places - fixed + turn * (used - fixed)) % max(1, number_of - fixed)
        return jnp.zeros((number_of,), jnp.int32).at[ranking[jnp.where(places < fixed, places, passed)]].set(jnp.asarray(tallies, jnp.int32))

    tallies = jnp.where(number % 4 == 0, named(packed, number // 4), named(usual, number - number // 4 - 1))
    mixed = jax.random.permutation(jax.random.fold_in(own, 3), number_of)
    donor, taker = mixed[0:number_of // 2 * 2:2], mixed[1:number_of // 2 * 2:2]
    room = jnp.minimum(tallies[donor] - 1, most - tallies[taker]) // 2
    room = jnp.where((donor == ranking[0]) | (taker == ranking[0]) | (tallies[taker] == 0), 0, jnp.maximum(room, 0))
    passed = jax.random.randint(jax.random.fold_in(own, 4), (number_of // 2,), 0, 1 << 20) % (room + 1)
    tallies = tallies.at[donor].add(-passed).at[taker].add(passed)
    items = jnp.searchsorted(jnp.cumsum(tallies), jnp.arange(rows * top), side="right").astype(jnp.int32)
    listing = items.reshape(top, rows).T
    listing = listing[jax.random.permutation(jax.random.fold_in(own, 1), rows)]
    turn = jax.random.randint(jax.random.fold_in(own, 2), (rows, 1), 0, top)
    return jnp.take_along_axis(listing, (jnp.arange(top)[None, :] + turn) % top, axis=1)


def portions_of(number_of, total, limit, lean, full):
    weights = [(1 << 20) // math.isqrt(rank ** lean) + 1 for rank in range(1, number_of + 1)]
    largest = limit if full else min(limit, max(-(-total // number_of), total * weights[0] // sum(weights)))
    least = 1 if total - largest >= number_of - 1 else 0
    counts, surplus = [largest] + [least] * (number_of - 1), total - largest - least * (number_of - 1)
    while surplus > 0:
        candidates = [i for i in range(1, number_of) if counts[i] < largest] or [i for i in range(1, number_of) if counts[i] < limit]
        pool, remaining = sum([weights[i] for i in candidates]), surplus
        for i in candidates:
            more = min(limit - counts[i], max(1, remaining * weights[i] // pool), surplus)
            counts[i] = counts[i] + more
            surplus = surplus - more
    return np.array(counts)


def bell_draw(own_key, extent, scale, most, split=(), held_as=jnp.bfloat16):
    values = jax.random.normal(own_key, extent, jnp.float32) * scale
    if len(split) > 0:
        values = shard_levels(own_key, extent, split, -0.22, 0.18) * values
    return jnp.clip(values, min=-most, max=most).astype(held_as)


def setup_inputs(seed: int = 0, part: int = 0) -> dict:
    arg_keys = jax.random.split(jax.random.key(seed), 11)
    part_splits = jax.random.split(jax.random.fold_in(arg_keys[10], part), 11)
    queries = draw_queries(jax.random.fold_in(jax.random.fold_in(arg_keys[10], part), 71), part)
    latent_cache = draw_latent_cache(jax.random.fold_in(jax.random.fold_in(arg_keys[10], part), 71), part)
    lengths = uneven(part_splits[2], REQUESTS, REQUESTS * CTX // 2, CTX, 2).astype(jnp.int32)
    trade_slot = place_ends(jax.random.randint(part_splits[3], (PAIRS,), 0, REQ_DEV), jax.random.fold_in(part_splits[3], 1), 0, REQ_DEV - 1).astype(jnp.int32)
    tokens = bell_draw(part_splits[4], (TOKENS, D), 1.0, 6.0, ((0, 32),))
    routing_keys = jax.random.split(jax.random.fold_in(part_splits[5], 1), TOKENS // TOK_DEV)
    routing_turns = jax.random.permutation(jax.random.fold_in(part_splits[5], 3), TOKENS // TOK_DEV)
    routing = jax.vmap(lambda own, number: assign_block(jax.random.fold_in(part_splits[5], 2), own, number, TOK_DEV, EXPERTS, TOP, CAP, 2))(routing_keys, routing_turns).reshape((TOKENS, TOP))
    gate_weights = jnp.clip(jnp.exp(math.log(0.5) - 2.3025851 * jax.random.uniform(part_splits[6], (TOKENS, TOP), jnp.float32) ** shard_levels(part_splits[6], (TOKENS, TOP), ((0, 32),), -0.2, 0.2)), 0.05, 0.5)
    w_gate = bell_draw(arg_keys[7], (EXPERTS, D, FF), D ** -0.5, 0.09375, ((0, 32),))
    w_up = bell_draw(arg_keys[8], (EXPERTS, D, FF), D ** -0.5, 0.09375, ((0, 32),))
    w_down = bell_draw(arg_keys[9], (EXPERTS, FF, D), FF ** -0.5, 0.1875, ((0, 32),))
    return dict(queries=queries, latent_cache=latent_cache, lengths=lengths, trade_slot=trade_slot, tokens=tokens, routing=routing, gate_weights=gate_weights, w_gate=w_gate, w_up=w_up, w_down=w_down)


score_scale = 192.0 ** -0.5


def reference(queries, latent_cache, lengths, trade_slot, tokens, routing, gate_weights, w_gate, w_up, w_down):
    half_way = N_DEV // 2
    request_ids = jnp.arange(REQUESTS, dtype=jnp.int32)
    holder = request_ids // REQ_DEV
    within = request_ids % REQ_DEV
    traded = within == trade_slot[holder % half_way]
    partner = (holder + half_way) % N_DEV
    source = jnp.where(traded, partner * REQ_DEV + within, request_ids).astype(jnp.int32)
    moved = latent_cache[source].astype(jnp.float32)
    live_len = lengths[source]
    scores = jnp.einsum("rhc,rkc->rhk", queries.astype(jnp.float32), moved) * score_scale
    position = jnp.arange(CTX, dtype=jnp.int32)
    visible = position[None, None, :] < live_len[:, None, None]
    scores = jnp.where(visible, scores, -jnp.inf)
    peak_score = jnp.max(scores, axis=2, keepdims=True)
    weights = jnp.exp(scores - peak_score)
    shares = (weights / jnp.sum(weights, axis=2, keepdims=True)).astype(jnp.bfloat16)
    attended = jnp.einsum("rhk,rkc->rhc", shares.astype(jnp.float32), moved[:, :, :LAT]).astype(jnp.bfloat16)

    def add_expert(carry, expert):
        gate = jnp.dot(tokens, w_gate[expert], preferred_element_type=jnp.float32)
        upward = jnp.dot(tokens, w_up[expert], preferred_element_type=jnp.float32)
        hidden = (jax.nn.silu(gate) * upward).astype(jnp.bfloat16)
        output = jnp.dot(hidden, w_down[expert], preferred_element_type=jnp.float32).astype(jnp.bfloat16)
        factor = jnp.sum(jnp.where(routing == expert, gate_weights, jnp.zeros_like(gate_weights)), axis=1)
        return carry + factor[:, None] * output.astype(jnp.float32), None

    summed, unused = lax.scan(add_expert, jnp.zeros((TOKENS, D), jnp.float32), jnp.arange(EXPERTS, dtype=jnp.int32))
    return attended, summed.astype(jnp.bfloat16)
```

```python
import functools

import jax
import jax.numpy as jnp
from jax import lax
from jax.experimental import pallas as pl
from jax.experimental.pallas import tpu as pltpu
from jax.sharding import PartitionSpec as P

LAT = 512
W = 512
PIECES = 7
SLOTS = 8
score_scale = 192.0 ** (-0.5)
MESH = pl.DeviceIdType.MESH
f32 = jnp.float32
bf16 = jnp.bfloat16


def send(src, dst, send_sem, recv_sem, to):
    return pltpu.make_async_remote_copy(
        src_ref=src,
        dst_ref=dst,
        send_sem=send_sem,
        recv_sem=recv_sem,
        device_id={"dev": to},
        device_id_type=MESH,
    )


def attend(q_t, k_t, live):
    scores = (
        lax.dot_general(q_t, k_t, (((0,), (0,)), ((), ())), preferred_element_type=f32)
        * score_scale
    )
    position = lax.broadcasted_iota(jnp.int32, scores.shape, 1)
    scores = jnp.where(position < live, scores, -jnp.inf)
    weights = jnp.exp(scores - jnp.max(scores, axis=1, keepdims=True))
    shares = (weights / jnp.sum(weights, axis=1, keepdims=True)).astype(bf16)
    return lax.dot_general(
        shares, k_t[:LAT], (((1,), (1,)), ((), ())), preferred_element_type=f32
    ).astype(bf16)


def kernel(
    q_hbm, k_hbm, lengths, trade_slot, tok_hbm, rout_hbm, gw_hbm, wg_hbm, wu_hbm, wd_hbm,
    att_hbm, exp_ref,
    tok, rout, gw, q, k, wg, wu, wd, stage, perm, gathered, q_out, q_in, o_out, o_in, att,
    sums, mate_in, back, landed,
    small_sem, q_sem, k_sem, wg_sem, wu_sem, wd_sem, att_sem,
    tok_s, tok_r, fwd_s, fwd_r, trade_s, trade_r, mate_s, mate_r, back_s, back_r,
):
    me = lax.axis_index("dev")
    chip, core = me // 2, me % 2
    cx, cz = chip // 4, chip % 4
    mate = chip * 2 + (1 - core)
    partner = (me + 16) % 32
    away = [(dx, dz) for dx in (2, 1, 3, 0) for dz in (2, 1, 3, 0) if (dx, dz) != (0, 0)]
    to_chip = [((cx + dx) % 4) * 4 + (cz + dz) % 4 for dx, dz in away]
    from_chip = [((cx + 4 - dx) % 4) * 4 + (cz + 4 - dz) % 4 for dx, dz in away]

    barrier = pltpu.get_barrier_semaphore()
    for other in [c * 2 + core for c in to_chip] + [mate]:
        pl.semaphore_signal(barrier, inc=1, device_id={"dev": other}, device_id_type=MESH)

    loads = [
        pltpu.make_async_copy(tok_hbm, tok, small_sem.at[0]),
        pltpu.make_async_copy(rout_hbm, rout, small_sem.at[1]),
        pltpu.make_async_copy(gw_hbm, gw, small_sem.at[2]),
        pltpu.make_async_copy(q_hbm, q, q_sem),
        pltpu.make_async_copy(k_hbm, k, k_sem),
    ]
    tok_load, rout_load, gw_load, q_load, k_load = loads
    wg_loads, wu_loads, wd_loads = [], [], []
    for s in range(PIECES):
        rows = pl.ds(s * W, W)
        wg_loads.append(pltpu.make_async_copy(wg_hbm.at[0, rows], wg.at[rows], wg_sem.at[s]))
        wu_loads.append(pltpu.make_async_copy(wu_hbm.at[0, rows], wu.at[rows], wu_sem.at[s]))
        wd_loads.append(
            pltpu.make_async_copy(wd_hbm.at[0, :, rows], wd.at[:, rows], wd_sem.at[s])
        )
    for load in loads:
        load.start()
    for s in range(PIECES):
        wg_loads[s].start()
        wu_loads[s].start()
    for s in range(PIECES):
        wd_loads[s].start()

    tok_load.wait()
    rout_load.wait()
    gw_load.wait()
    tokens = tok[...].astype(f32)
    lane = lax.broadcasted_iota(jnp.int32, (2, W), 1)
    factor = jnp.zeros((2, W), f32)
    for top in range(8):
        expert, weight = rout[:, top : top + 1], gw[:, top : top + 1]
        hit = (lane == expert) | (lane == expert + 32)
        factor = factor + jnp.where(hit, weight, 0.0)
    high = factor.astype(bf16).astype(f32)
    factor = jnp.where(lane < 32, high, factor - high)
    for t in range(2):
        for s in range(PIECES):
            stage[t * SLOTS + s : t * SLOTS + s + 1, :] = tokens[t : t + 1, s * W : (s + 1) * W]
        stage[t * SLOTS + PIECES : (t + 1) * SLOTS, :] = factor[t : t + 1]
    gathered[core, chip] = stage[...].astype(bf16)

    pl.semaphore_wait(barrier, 16)

    own = gathered.at[core, chip]
    tok_copies = [
        send(own, own, tok_s.at[i], tok_r.at[i], to_chip[i] * 2 + core) for i in range(15)
    ]
    own_copy = send(own, own, fwd_s.at[15], fwd_r.at[15], mate)
    for copy in tok_copies:
        copy.start()
    own_copy.start()

    trade_at = trade_slot[me % 16]
    keep_at = 1 - trade_at
    q_load.wait()
    q_out[...] = q[trade_at]
    q_copy = send(q_out, q_in, trade_s.at[0], trade_r.at[0], partner)
    q_copy.start()

    row = lax.broadcasted_iota(jnp.int32, (512, 512), 0)
    col = lax.broadcasted_iota(jnp.int32, (512, 512), 1)
    perm[...] = jnp.where(col == (row % 64) * SLOTS + row // 64, 1.0, 0.0).astype(bf16)

    k_load.wait()
    kept = attend(q[keep_at], k[keep_at], lengths[me * 2 + keep_at])

    fwd_copies = []
    for i in range(15):
        tok_copies[i].wait_recv()
        block = gathered.at[core, from_chip[i]]
        fwd_copies.append(send(block, block, fwd_s.at[i], fwd_r.at[i], mate))
        fwd_copies[i].start()

    q_copy.wait_recv()
    o_out[...] = attend(q_in[...], k[trade_at], lengths[me * 2 + trade_at])
    o_copy = send(o_out, o_in, trade_s.at[1], trade_r.at[1], partner)
    o_copy.start()

    for copy in fwd_copies + [own_copy]:
        copy.wait_recv()
    rows = gathered[...].reshape(512, W)

    gate = jnp.zeros((64, 1024), f32)
    up = jnp.zeros((64, 1024), f32)
    for s in range(PIECES):
        x = jnp.dot(perm[s * 64 : (s + 1) * 64, :], rows, preferred_element_type=f32).astype(bf16)
        wg_loads[s].wait()
        gate += jnp.dot(x, wg[s * W : (s + 1) * W, :], preferred_element_type=f32)
        wu_loads[s].wait()
        up += jnp.dot(x, wu[s * W : (s + 1) * W, :], preferred_element_type=f32)
    factors = jnp.dot(perm[PIECES * 64 :, :], rows, preferred_element_type=f32)
    lane = lax.broadcasted_iota(jnp.int32, (64, W), 1)
    mine = (lane == me) | (lane == me + 32)
    weight = jnp.sum(jnp.where(mine, factors, 0.0), axis=1, keepdims=True)
    hidden = (gate / (1.0 + jnp.exp(-gate)) * up).astype(bf16)

    mate_copies = []
    for s in range(PIECES):
        wd_loads[s].wait()
        y = jnp.dot(hidden, wd[:, s * W : (s + 1) * W], preferred_element_type=f32).astype(bf16)
        sums[s] = (y.astype(f32) * weight).astype(bf16).reshape(2, 32, W)
        mate_copies.append(
            send(sums.at[s, 1 - core], mate_in.at[s], mate_s.at[s], mate_r.at[s], mate)
        )
        mate_copies[s].start()
    parts = []
    for s in range(PIECES):
        mate_copies[s].wait_recv()
        parts.append((sums[s, core].astype(f32) + mate_in[s].astype(f32)).astype(bf16))
    parts.append(jnp.zeros((32, W), bf16))
    row = lax.broadcasted_iota(jnp.int32, (256, 256), 0)
    col = lax.broadcasted_iota(jnp.int32, (256, 256), 1)
    unperm = jnp.where(col == (row % SLOTS) * 32 + row // SLOTS, 1.0, 0.0).astype(bf16)
    back[...] = (
        jnp.dot(unperm, jnp.concatenate(parts, axis=0), preferred_element_type=f32)
        .astype(bf16)
        .reshape(16, 16, W)
    )
    back_copies = [
        send(
            back.at[to_chip[i]], landed.at[chip], back_s.at[i], back_r.at[i], to_chip[i] * 2 + core
        )
        for i in range(15)
    ]
    for copy in back_copies:
        copy.start()
    landed[chip] = back[chip]

    o_copy.wait_recv()
    arrived = o_in[...]
    att[0] = jnp.where(trade_at == 0, arrived, kept)
    att[1] = jnp.where(trade_at == 1, arrived, kept)
    att_copy = pltpu.make_async_copy(att, att_hbm, att_sem)
    att_copy.start()

    for copy in back_copies:
        copy.wait_recv()
    total = landed[0].astype(f32)
    for c in range(1, 16):
        total += landed[c].astype(f32)
    exp_ref[...] = total.astype(bf16)

    att_copy.wait()
    for copy in tok_copies + fwd_copies + mate_copies + back_copies + [own_copy, q_copy, o_copy]:
        copy.wait_send()


def local(
    queries, latent_cache, lengths, trade_slot, tokens, routing, gate_weights, w_gate, w_up, w_down
):
    any_spec = pl.BlockSpec(memory_space=pl.ANY)
    smem_spec = pl.BlockSpec(memory_space=pltpu.SMEM)
    dma = pltpu.SemaphoreType.DMA
    vmem = pltpu.VMEM
    attended, rows = pl.pallas_call(
        kernel,
        out_shape=(
            jax.ShapeDtypeStruct((2, 128, LAT), bf16),
            jax.ShapeDtypeStruct((16, W), bf16),
        ),
        in_specs=[any_spec, any_spec, smem_spec, smem_spec] + [any_spec] * 6,
        out_specs=(any_spec, pl.BlockSpec(memory_space=pltpu.VMEM)),
        scratch_shapes=[
            vmem((2, 3584), bf16),
            vmem((2, 8), jnp.int32),
            vmem((2, 8), f32),
            vmem((2, 576, 128), bf16),
            vmem((2, 576, 1024), bf16),
            vmem((3584, 1024), bf16),
            vmem((3584, 1024), bf16),
            vmem((1024, 3584), bf16),
            vmem((16, W), f32),
            vmem((512, 512), bf16),
            vmem((2, 16, 16, W), bf16),
            vmem((576, 128), bf16),
            vmem((576, 128), bf16),
            vmem((128, LAT), bf16),
            vmem((128, LAT), bf16),
            vmem((2, 128, LAT), bf16),
            vmem((PIECES, 2, 32, W), bf16),
            vmem((PIECES, 32, W), bf16),
            vmem((16, 16, W), bf16),
            vmem((16, 16, W), bf16),
            dma((3,)),
            dma,
            dma,
            dma((PIECES,)),
            dma((PIECES,)),
            dma((PIECES,)),
            dma,
            dma((15,)),
            dma((15,)),
            dma((16,)),
            dma((16,)),
            dma((2,)),
            dma((2,)),
            dma((PIECES,)),
            dma((PIECES,)),
            dma((15,)),
            dma((15,)),
        ],
        compiler_params=pltpu.CompilerParams(
            collective_id=0, has_side_effects=True, vmem_limit_bytes=50 * 2**20
        ),
        cost_estimate=pl.CostEstimate(
            flops=2_000_000_000, bytes_accessed=25_000_000, transcendentals=400_000
        ),
    )(
        jnp.swapaxes(queries, 1, 2),
        jnp.swapaxes(latent_cache, 1, 2),
        lengths,
        trade_slot,
        tokens,
        routing,
        gate_weights,
        w_gate,
        w_up,
        w_down,
    )
    expert_out = rows.reshape(2, SLOTS, W)[:, :PIECES].reshape(2, PIECES * W)
    return attended, expert_out


def solution(mesh):
    in_specs = (
        P(("rep", "dev"), None, None),
        P(("rep", "dev"), None, None),
        P("rep"),
        P("rep"),
        P(("rep", "dev"), None),
        P(("rep", "dev"), None),
        P(("rep", "dev"), None),
        P("dev", None, None),
        P("dev", None, None),
        P("dev", None, None),
    )
    out_specs = (P(("rep", "dev"), None, None), P(("rep", "dev"), None))
    return jax.shard_map(local, mesh=mesh, in_specs=in_specs, out_specs=out_specs, check_vma=False)
```

```python
import functools

import jax
import jax.numpy as jnp
from jax import lax
from jax.experimental import pallas as pl
from jax.experimental.pallas import tpu as pltpu
from jax.sharding import PartitionSpec as P

LAT = 512
W = 512
PIECES = 7
SLOTS = 8
score_scale = 192.0 ** (-0.5)
MESH = pl.DeviceIdType.MESH
f32 = jnp.float32
bf16 = jnp.bfloat16


def send(src, dst, send_sem, recv_sem, to):
    return pltpu.make_async_remote_copy(
        src_ref=src,
        dst_ref=dst,
        send_sem=send_sem,
        recv_sem=recv_sem,
        device_id={"dev": to},
        device_id_type=MESH,
    )


def attend(q_t, k_t, live):
    scores = (
        lax.dot_general(q_t, k_t, (((0,), (0,)), ((), ())), preferred_element_type=f32)
        * score_scale
    )
    position = lax.broadcasted_iota(jnp.int32, scores.shape, 1)
    scores = jnp.where(position < live, scores, -jnp.inf)
    weights = jnp.exp(scores - jnp.max(scores, axis=1, keepdims=True))
    shares = (weights / jnp.sum(weights, axis=1, keepdims=True)).astype(bf16)
    return lax.dot_general(
        shares, k_t[:LAT], (((1,), (1,)), ((), ())), preferred_element_type=f32
    ).astype(bf16)


def kernel(
    q_hbm, k_hbm, len_hbm, trade_hbm, tok_hbm, rout_hbm, gw_hbm, wg_hbm, wu_hbm, wd_hbm,
    att_hbm, exp_ref,
    lengths, trade_slot, tok, rout, gw, q, k, wg, wu, wd, stage, perm, gathered, tok_rows, q_out, q_in, o_out, o_in, att,
    sums, mate_in, back, landed,
    small_sem, q_sem, k_sem, wg_sem, wu_sem, wd_sem, att_sem,
    tok_s, tok_r, fwd_s, fwd_r, trade_s, trade_r, mate_s, mate_r, back_s, back_r,
):
    me = lax.axis_index("dev")
    chip, core = me // 2, me % 2
    cx, cz = chip // 4, chip % 4
    mate = chip * 2 + (1 - core)
    partner = (me + 16) % 32
    away = [(dx, dz) for dx in (2, 1, 3, 0) for dz in (2, 1, 3, 0) if (dx, dz) != (0, 0)]
    to_chip = [((cx + dx) % 4) * 4 + (cz + dz) % 4 for dx, dz in away]
    from_chip = [((cx + 4 - dx) % 4) * 4 + (cz + 4 - dz) % 4 for dx, dz in away]

    barrier = pltpu.get_barrier_semaphore()
    for other in [c * 2 + core for c in to_chip] + [mate]:
        pl.semaphore_signal(barrier, inc=1, device_id={"dev": other}, device_id_type=MESH)

    loads = [
        pltpu.make_async_copy(tok_hbm, tok, small_sem.at[0]),
        pltpu.make_async_copy(rout_hbm, rout, small_sem.at[1]),
        pltpu.make_async_copy(gw_hbm, gw, small_sem.at[2]),
        pltpu.make_async_copy(trade_hbm, trade_slot, small_sem.at[3]),
        pltpu.make_async_copy(len_hbm, lengths, small_sem.at[4]),
        pltpu.make_async_copy(q_hbm, q, q_sem),
        pltpu.make_async_copy(k_hbm, k, k_sem),
    ]
    tok_load, rout_load, gw_load, trade_load, len_load, q_load, k_load = loads
    wg_loads, wu_loads, wd_loads = [], [], []
    for s in range(PIECES):
        rows = pl.ds(s * W, W)
        wg_loads.append(pltpu.make_async_copy(wg_hbm.at[0, rows], wg.at[rows], wg_sem.at[s]))
        wu_loads.append(pltpu.make_async_copy(wu_hbm.at[0, rows], wu.at[rows], wu_sem.at[s]))
        wd_loads.append(
            pltpu.make_async_copy(wd_hbm.at[0, :, rows], wd.at[:, rows], wd_sem.at[s])
        )
    for load in loads:
        load.start()
    for s in range(PIECES):
        wg_loads[s].start()
        wu_loads[s].start()
    for s in range(PIECES):
        wd_loads[s].start()

    tok_load.wait()
    rout_load.wait()
    gw_load.wait()
    tokens = tok[...].astype(f32)
    lane = lax.broadcasted_iota(jnp.int32, (2, W), 1)
    factor = jnp.zeros((2, W), f32)
    for top in range(8):
        expert, weight = rout[:, top : top + 1], gw[:, top : top + 1]
        hit = (lane == expert) | (lane == expert + 32)
        factor = factor + jnp.where(hit, weight, 0.0)
    high = factor.astype(bf16).astype(f32)
    factor = jnp.where(lane < 32, high, factor - high)
    for t in range(2):
        for s in range(PIECES):
            stage[t * SLOTS + s : t * SLOTS + s + 1, :] = tokens[t : t + 1, s * W : (s + 1) * W]
        stage[t * SLOTS + PIECES : (t + 1) * SLOTS, :] = factor[t : t + 1]
    gathered[core, chip] = stage[...].astype(bf16)

    pl.semaphore_wait(barrier, 16)

    own = gathered.at[core, chip]
    tok_copies = [
        send(own, own, tok_s.at[i], tok_r.at[i], to_chip[i] * 2 + core) for i in range(15)
    ]
    own_copy = send(own, own, fwd_s.at[15], fwd_r.at[15], mate)
    for copy in tok_copies:
        copy.start()
    own_copy.start()

    trade_load.wait()
    len_load.wait()
    trade_at = trade_slot[me % 16]
    keep_at = 1 - trade_at
    q_load.wait()
    q_out[...] = q[trade_at]
    q_copy = send(q_out, q_in, trade_s.at[0], trade_r.at[0], partner)
    q_copy.start()

    row = lax.broadcasted_iota(jnp.int32, (512, 512), 0)
    col = lax.broadcasted_iota(jnp.int32, (512, 512), 1)
    perm[...] = jnp.where(col == (row % 64) * SLOTS + row // 64, 1.0, 0.0).astype(bf16)

    k_load.wait()
    kept = attend(q[keep_at], k[keep_at], lengths[me * 2 + keep_at])

    fwd_copies = []
    for i in range(15):
        tok_copies[i].wait_recv()
        block = gathered.at[core, from_chip[i]]
        fwd_copies.append(send(block, block, fwd_s.at[i], fwd_r.at[i], mate))
        fwd_copies[i].start()

    for copy in fwd_copies + [own_copy]:
        copy.wait_recv()
    rows = jnp.dot(perm[...], gathered[...].reshape(512, W), preferred_element_type=f32)
    for s in range(PIECES):
        tok_rows[s] = rows[s * 64 : (s + 1) * 64].astype(bf16)
    lane = lax.broadcasted_iota(jnp.int32, (64, W), 1)
    mine = (lane == me) | (lane == me + 32)
    weight = jnp.sum(jnp.where(mine, rows[PIECES * 64 :], 0.0), axis=1, keepdims=True)

    gate = jnp.zeros((64, 1024), f32)
    up = jnp.zeros((64, 1024), f32)
    for s in range(PIECES):
        wg_loads[s].wait()
        gate += jnp.dot(tok_rows[s], wg[s * W : (s + 1) * W, :], preferred_element_type=f32)
        wu_loads[s].wait()
        up += jnp.dot(tok_rows[s], wu[s * W : (s + 1) * W, :], preferred_element_type=f32)
    hidden = (gate / (1.0 + jnp.exp(-gate)) * up).astype(bf16)

    q_copy.wait_recv()
    o_out[...] = attend(q_in[...], k[trade_at], lengths[me * 2 + trade_at])
    o_copy = send(o_out, o_in, trade_s.at[1], trade_r.at[1], partner)
    o_copy.start()

    mate_copies = []
    for s in range(PIECES):
        wd_loads[s].wait()
        y = jnp.dot(hidden, wd[:, s * W : (s + 1) * W], preferred_element_type=f32).astype(bf16)
        sums[s] = (y.astype(f32) * weight).astype(bf16).reshape(2, 32, W)
        mate_copies.append(
            send(sums.at[s, 1 - core], mate_in.at[s], mate_s.at[s], mate_r.at[s], mate)
        )
        mate_copies[s].start()
    parts = []
    for s in range(PIECES):
        mate_copies[s].wait_recv()
        parts.append((sums[s, core].astype(f32) + mate_in[s].astype(f32)).astype(bf16))
    parts.append(jnp.zeros((32, W), bf16))
    row = lax.broadcasted_iota(jnp.int32, (256, 256), 0)
    col = lax.broadcasted_iota(jnp.int32, (256, 256), 1)
    unperm = jnp.where(col == (row % SLOTS) * 32 + row // SLOTS, 1.0, 0.0).astype(bf16)
    back[...] = (
        jnp.dot(unperm, jnp.concatenate(parts, axis=0), preferred_element_type=f32)
        .astype(bf16)
        .reshape(16, 16, W)
    )
    back_copies = [
        send(
            back.at[to_chip[i]], landed.at[chip], back_s.at[i], back_r.at[i], to_chip[i] * 2 + core
        )
        for i in range(15)
    ]
    for copy in back_copies:
        copy.start()
    landed[chip] = back[chip]
    o_copy.wait_recv()
    arrived = o_in[...]
    att[0] = jnp.where(trade_at == 0, arrived, kept)
    att[1] = jnp.where(trade_at == 1, arrived, kept)
    att_copy = pltpu.make_async_copy(att, att_hbm, att_sem)
    att_copy.start()

    for copy in back_copies:
        copy.wait_recv()
    total = landed[0].astype(f32)
    for c in range(1, 16):
        total += landed[c].astype(f32)
    exp_ref[...] = total.astype(bf16)

    att_copy.wait()
    for copy in tok_copies + fwd_copies + mate_copies + back_copies + [own_copy, q_copy, o_copy]:
        copy.wait_send()


def local(
    queries, latent_cache, lengths, trade_slot, tokens, routing, gate_weights, w_gate, w_up, w_down
):
    hbm_spec = pl.BlockSpec(memory_space=pltpu.HBM)
    dma = pltpu.SemaphoreType.DMA
    vmem = pltpu.VMEM
    attended, rows = pl.pallas_call(
        kernel,
        out_shape=(
            jax.ShapeDtypeStruct((2, 128, LAT), bf16),
            jax.ShapeDtypeStruct((16, W), bf16),
        ),
        in_specs=[hbm_spec] * 10,
        out_specs=(pl.BlockSpec(memory_space=pl.ANY), pl.BlockSpec(memory_space=pltpu.VMEM)),
        scratch_shapes=[
            pltpu.SMEM((64,), jnp.int32),
            pltpu.SMEM((16,), jnp.int32),
            vmem((2, 3584), bf16),
            vmem((2, 8), jnp.int32),
            vmem((2, 8), f32),
            vmem((2, 576, 128), bf16),
            vmem((2, 576, 1024), bf16),
            vmem((3584, 1024), bf16),
            vmem((3584, 1024), bf16),
            vmem((1024, 3584), bf16),
            vmem((16, W), f32),
            vmem((512, 512), bf16),
            vmem((2, 16, 16, W), bf16),
            vmem((PIECES, 64, W), bf16),
            vmem((576, 128), bf16),
            vmem((576, 128), bf16),
            vmem((128, LAT), bf16),
            vmem((128, LAT), bf16),
            vmem((2, 128, LAT), bf16),
            vmem((PIECES, 2, 32, W), bf16),
            vmem((PIECES, 32, W), bf16),
            vmem((16, 16, W), bf16),
            vmem((16, 16, W), bf16),
            dma((5,)),
            dma,
            dma,
            dma((PIECES,)),
            dma((PIECES,)),
            dma((PIECES,)),
            dma,
            dma((15,)),
            dma((15,)),
            dma((16,)),
            dma((16,)),
            dma((2,)),
            dma((2,)),
            dma((PIECES,)),
            dma((PIECES,)),
            dma((15,)),
            dma((15,)),
        ],
        compiler_params=pltpu.CompilerParams(
            collective_id=0, has_side_effects=True, vmem_limit_bytes=56 * 2**20
        ),
        cost_estimate=pl.CostEstimate(
            flops=2_000_000_000, bytes_accessed=25_000_000, transcendentals=400_000
        ),
    )(
        jnp.swapaxes(queries, 1, 2),
        jnp.swapaxes(latent_cache, 1, 2),
        lengths,
        trade_slot,
        tokens,
        routing,
        gate_weights,
        w_gate,
        w_up,
        w_down,
    )
    expert_out = rows.reshape(2, SLOTS, W)[:, :PIECES].reshape(2, PIECES * W)
    return attended, expert_out


def solution(mesh):
    in_specs = (
        P(("rep", "dev"), None, None),
        P(("rep", "dev"), None, None),
        P("rep"),
        P("rep"),
        P(("rep", "dev"), None),
        P(("rep", "dev"), None),
        P(("rep", "dev"), None),
        P("dev", None, None),
        P("dev", None, None),
        P("dev", None, None),
    )
    out_specs = (P(("rep", "dev"), None, None), P(("rep", "dev"), None))
    return jax.shard_map(local, mesh=mesh, in_specs=in_specs, out_specs=out_specs, check_vma=False)
```

```python
import functools

import jax
import jax.numpy as jnp
from jax import lax
from jax.experimental import pallas as pl
from jax.experimental.pallas import tpu as pltpu
from jax.sharding import PartitionSpec as P

LAT = 512
W = 512
PIECES = 7
SLOTS = 8
score_scale = 192.0 ** (-0.5)
MESH = pl.DeviceIdType.MESH
f32 = jnp.float32
bf16 = jnp.bfloat16


def send(src, dst, send_sem, recv_sem, to):
    return pltpu.make_async_remote_copy(
        src_ref=src,
        dst_ref=dst,
        send_sem=send_sem,
        recv_sem=recv_sem,
        device_id={"dev": to},
        device_id_type=MESH,
    )


def attend(q_t, k_t, live):
    scores = (
        lax.dot_general(q_t, k_t, (((0,), (0,)), ((), ())), preferred_element_type=f32)
        * score_scale
    )
    position = lax.broadcasted_iota(jnp.int32, scores.shape, 1)
    scores = jnp.where(position < live, scores, -jnp.inf)
    weights = jnp.exp(scores - jnp.max(scores, axis=1, keepdims=True))
    shares = (weights / jnp.sum(weights, axis=1, keepdims=True)).astype(bf16)
    return lax.dot_general(
        shares, k_t[:LAT], (((1,), (1,)), ((), ())), preferred_element_type=f32
    ).astype(bf16)


def kernel(
    q_hbm, k_hbm, len_hbm, trade_hbm, tok_hbm, rout_hbm, gw_hbm, wg_hbm, wu_hbm, wd_hbm,
    att, exp_ref,
    lengths, trade_slot, tok, rout, gw, q, k, wg, wu, wd, stage, perm, gathered, tok_rows, q_out, q_in, o_out, o_in,
    sums, mate_in, back, landed,
    small_sem, q_sem, k_sem, wg_sem, wu_sem, wd_sem,
    tok_s, tok_r, fwd_s, fwd_r, trade_s, trade_r, mate_s, mate_r, back_s, back_r,
):
    me = lax.axis_index("dev")
    chip, core = me // 2, me % 2
    cx, cz = chip // 4, chip % 4
    mate = chip * 2 + (1 - core)
    partner = (me + 16) % 32
    away = [(dx, dz) for dx in (2, 1, 3, 0) for dz in (2, 1, 3, 0) if (dx, dz) != (0, 0)]
    to_chip = [((cx + dx) % 4) * 4 + (cz + dz) % 4 for dx, dz in away]
    from_chip = [((cx + 4 - dx) % 4) * 4 + (cz + 4 - dz) % 4 for dx, dz in away]

    barrier = pltpu.get_barrier_semaphore()
    loads = [
        pltpu.make_async_copy(tok_hbm, tok, small_sem.at[0]),
        pltpu.make_async_copy(rout_hbm, rout, small_sem.at[1]),
        pltpu.make_async_copy(gw_hbm, gw, small_sem.at[2]),
        pltpu.make_async_copy(trade_hbm, trade_slot, small_sem.at[3]),
        pltpu.make_async_copy(len_hbm, lengths, small_sem.at[4]),
        pltpu.make_async_copy(q_hbm, q, q_sem),
        pltpu.make_async_copy(k_hbm, k, k_sem),
    ]
    tok_load, rout_load, gw_load, trade_load, len_load, q_load, k_load = loads
    wg_loads, wu_loads, wd_loads = [], [], []
    for s in range(PIECES):
        rows = pl.ds(s * W, W)
        wg_loads.append(pltpu.make_async_copy(wg_hbm.at[0, rows], wg.at[rows], wg_sem.at[s]))
        wu_loads.append(pltpu.make_async_copy(wu_hbm.at[0, rows], wu.at[rows], wu_sem.at[s]))
        wd_loads.append(
            pltpu.make_async_copy(wd_hbm.at[0, :, rows], wd.at[:, rows], wd_sem.at[s])
        )
    for load in loads[:3]:
        load.start()
    for other in [c * 2 + core for c in to_chip] + [mate]:
        pl.semaphore_signal(barrier, inc=1, device_id={"dev": other}, device_id_type=MESH)
    for load in loads[3:]:
        load.start()

    tok_load.wait()
    rout_load.wait()
    gw_load.wait()
    tokens = tok[...].astype(f32)
    lane = lax.broadcasted_iota(jnp.int32, (2, W), 1)
    factor = jnp.zeros((2, W), f32)
    for top in range(8):
        expert, weight = rout[:, top : top + 1], gw[:, top : top + 1]
        hit = (lane == expert) | (lane == expert + 32)
        factor = factor + jnp.where(hit, weight, 0.0)
    high = factor.astype(bf16).astype(f32)
    factor = jnp.where(lane < 32, high, factor - high)
    for t in range(2):
        for s in range(PIECES):
            stage[t * SLOTS + s : t * SLOTS + s + 1, :] = tokens[t : t + 1, s * W : (s + 1) * W]
        stage[t * SLOTS + PIECES : (t + 1) * SLOTS, :] = factor[t : t + 1]
    gathered[core, chip] = stage[...].astype(bf16)
    for s in range(PIECES):
        wg_loads[s].start()
        wu_loads[s].start()

    pl.semaphore_wait(barrier, 16)

    own = gathered.at[core, chip]
    tok_copies = [
        send(own, own, tok_s.at[i], tok_r.at[i], to_chip[i] * 2 + core) for i in range(15)
    ]
    for copy in tok_copies:
        copy.start()

    trade_load.wait()
    len_load.wait()
    trade_at = trade_slot[me % 16]
    keep_at = 1 - trade_at
    q_load.wait()
    q_out[...] = q[trade_at]
    q_copy = send(q_out, q_in, trade_s.at[0], trade_r.at[0], partner)
    q_copy.start()

    row = lax.broadcasted_iota(jnp.int32, (512, 512), 0)
    col = lax.broadcasted_iota(jnp.int32, (512, 512), 1)
    perm[...] = jnp.where(col == (row % 64) * SLOTS + row // 64, 1.0, 0.0).astype(bf16)

    k_load.wait()
    kept = attend(q[keep_at], k[keep_at], lengths[me * 2 + keep_at])

    for s in range(PIECES):
        wd_loads[s].start()
    for copy in tok_copies:
        copy.wait_recv()
    mine = gathered.at[core]
    fwd_copies = [send(mine, mine, fwd_s.at[0], fwd_r.at[0], mate)]
    fwd_copies[0].start()

    for copy in fwd_copies:
        copy.wait_recv()
    rows = jnp.dot(perm[...], gathered[...].reshape(512, W), preferred_element_type=f32)
    for s in range(PIECES):
        tok_rows[s] = rows[s * 64 : (s + 1) * 64].astype(bf16)
    lane = lax.broadcasted_iota(jnp.int32, (64, W), 1)
    mine = (lane == me) | (lane == me + 32)
    weight = jnp.sum(jnp.where(mine, rows[PIECES * 64 :], 0.0), axis=1, keepdims=True)

    gate = jnp.zeros((64, 1024), f32)
    up = jnp.zeros((64, 1024), f32)
    for s in range(PIECES):
        wg_loads[s].wait()
        gate += jnp.dot(tok_rows[s], wg[s * W : (s + 1) * W, :], preferred_element_type=f32)
        wu_loads[s].wait()
        up += jnp.dot(tok_rows[s], wu[s * W : (s + 1) * W, :], preferred_element_type=f32)
    hidden = (gate / (1.0 + jnp.exp(-gate)) * up).astype(bf16)

    q_copy.wait_recv()
    o_out[...] = attend(q_in[...], k[trade_at], lengths[me * 2 + trade_at])
    o_copy = send(o_out, o_in, trade_s.at[1], trade_r.at[1], partner)
    o_copy.start()

    mate_copies = []
    for s in range(PIECES):
        wd_loads[s].wait()
        y = jnp.dot(hidden, wd[:, s * W : (s + 1) * W], preferred_element_type=f32).astype(bf16)
        sums[s] = (y.astype(f32) * weight).astype(bf16).reshape(2, 32, W)
        mate_copies.append(
            send(sums.at[s, 1 - core], mate_in.at[s], mate_s.at[s], mate_r.at[s], mate)
        )
        mate_copies[s].start()
    parts = []
    for s in range(PIECES):
        mate_copies[s].wait_recv()
        parts.append((sums[s, core].astype(f32) + mate_in[s].astype(f32)).astype(bf16))
    parts.append(jnp.zeros((32, W), bf16))
    row = lax.broadcasted_iota(jnp.int32, (256, 256), 0)
    col = lax.broadcasted_iota(jnp.int32, (256, 256), 1)
    unperm = jnp.where(col == (row % SLOTS) * 32 + row // SLOTS, 1.0, 0.0).astype(bf16)
    back[...] = (
        jnp.dot(unperm, jnp.concatenate(parts, axis=0), preferred_element_type=f32)
        .astype(bf16)
        .reshape(16, 16, W)
    )
    back_copies = [
        send(
            back.at[to_chip[i]], landed.at[chip], back_s.at[i], back_r.at[i], to_chip[i] * 2 + core
        )
        for i in range(15)
    ]
    for copy in back_copies:
        copy.start()
    landed[chip] = back[chip]
    o_copy.wait_recv()
    arrived = o_in[...]
    att[0] = jnp.where(trade_at == 0, arrived, kept)
    att[1] = jnp.where(trade_at == 1, arrived, kept)

    for copy in back_copies:
        copy.wait_recv()
    total = landed[0].astype(f32)
    for c in range(1, 16):
        total += landed[c].astype(f32)
    exp_ref[...] = total.astype(bf16)

    for copy in tok_copies + fwd_copies + mate_copies + back_copies + [q_copy, o_copy]:
        copy.wait_send()


def local(
    queries, latent_cache, lengths, trade_slot, tokens, routing, gate_weights, w_gate, w_up, w_down
):
    hbm_spec = pl.BlockSpec(memory_space=pltpu.HBM)
    dma = pltpu.SemaphoreType.DMA
    vmem = pltpu.VMEM
    attended, rows = pl.pallas_call(
        kernel,
        out_shape=(
            pltpu.VMEM((2, 128, LAT), bf16),
            pltpu.VMEM((16, W), bf16),
        ),
        in_specs=[hbm_spec] * 10,
        out_specs=(pl.BlockSpec(memory_space=pltpu.VMEM),) * 2,
        scratch_shapes=[
            pltpu.SMEM((64,), jnp.int32),
            pltpu.SMEM((16,), jnp.int32),
            vmem((2, 3584), bf16),
            vmem((2, 8), jnp.int32),
            vmem((2, 8), f32),
            vmem((2, 576, 128), bf16),
            vmem((2, 576, 1024), bf16),
            vmem((3584, 1024), bf16),
            vmem((3584, 1024), bf16),
            vmem((1024, 3584), bf16),
            vmem((16, W), f32),
            vmem((512, 512), bf16),
            vmem((2, 16, 16, W), bf16),
            vmem((PIECES, 64, W), bf16),
            vmem((576, 128), bf16),
            vmem((576, 128), bf16),
            vmem((128, LAT), bf16),
            vmem((128, LAT), bf16),
            vmem((PIECES, 2, 32, W), bf16),
            vmem((PIECES, 32, W), bf16),
            vmem((16, 16, W), bf16),
            vmem((16, 16, W), bf16),
            dma((5,)),
            dma,
            dma,
            dma((PIECES,)),
            dma((PIECES,)),
            dma((PIECES,)),
            dma((15,)),
            dma((15,)),
            dma((16,)),
            dma((16,)),
            dma((2,)),
            dma((2,)),
            dma((PIECES,)),
            dma((PIECES,)),
            dma((15,)),
            dma((15,)),
        ],
        compiler_params=pltpu.CompilerParams(
            collective_id=0, has_side_effects=True, vmem_limit_bytes=56 * 2**20
        ),
        cost_estimate=pl.CostEstimate(
            flops=2_000_000_000, bytes_accessed=25_000_000, transcendentals=400_000
        ),
    )(
        *[
            pltpu.with_memory_space_constraint(operand, pltpu.HBM)
            for operand in (
                jnp.swapaxes(queries, 1, 2),
                jnp.swapaxes(latent_cache, 1, 2),
                lengths,
                trade_slot,
                tokens,
                routing,
                gate_weights,
                w_gate,
                w_up,
                w_down,
            )
        ]
    )
    expert_out = rows.reshape(2, SLOTS, W)[:, :PIECES].reshape(2, PIECES * W)
    return attended, expert_out


def solution(mesh):
    in_specs = (
        P(("rep", "dev"), None, None),
        P(("rep", "dev"), None, None),
        P("rep"),
        P("rep"),
        P(("rep", "dev"), None),
        P(("rep", "dev"), None),
        P(("rep", "dev"), None),
        P("dev", None, None),
        P("dev", None, None),
        P("dev", None, None),
    )
    out_specs = (P(("rep", "dev"), None, None), P(("rep", "dev"), None))
    return jax.shard_map(local, mesh=mesh, in_specs=in_specs, out_specs=out_specs, check_vma=False)
```

```python
import functools

import jax
import jax.numpy as jnp
from jax import lax
from jax.experimental import pallas as pl
from jax.experimental.pallas import tpu as pltpu
from jax.sharding import PartitionSpec as P

LAT = 512
W = 512
CUTS = ((0, 4), (4, 7))
BATCHES = ((0, 16),)
PIECES = 7
SLOTS = 8
score_scale = 192.0 ** (-0.5)
MESH = pl.DeviceIdType.MESH
f32 = jnp.float32
bf16 = jnp.bfloat16


def send(src, dst, send_sem, recv_sem, to):
    return pltpu.make_async_remote_copy(
        src_ref=src,
        dst_ref=dst,
        send_sem=send_sem,
        recv_sem=recv_sem,
        device_id={"dev": to},
        device_id_type=MESH,
    )


def attend(q_t, k_t, live):
    scores = (
        lax.dot_general(q_t, k_t, (((0,), (0,)), ((), ())), preferred_element_type=f32)
        * score_scale
    )
    position = lax.broadcasted_iota(jnp.int32, scores.shape, 1)
    scores = jnp.where(position < live, scores, -jnp.inf)
    weights = jnp.exp(scores - jnp.max(scores, axis=1, keepdims=True))
    shares = (weights / jnp.sum(weights, axis=1, keepdims=True)).astype(bf16)
    return lax.dot_general(
        shares, k_t[:LAT], (((1,), (1,)), ((), ())), preferred_element_type=f32
    ).astype(bf16)


def kernel(
    q_hbm, k_hbm, len_hbm, trade_hbm, tok_hbm, rout_hbm, gw_hbm, wg_hbm, wu_hbm, wd_hbm,
    att, exp_ref,
    lengths, trade_slot, tok, rout, gw, q, k, wg, wu, wd, stage, perm, gathered, tok_rows, factors,
    q_out, q_in, o_out, o_in, sums, mate_in, back, landed,
    small_sem, q_sem, k_sem, wg_sem, wu_sem, wd_sem,
    tok_s, tok_r, fwd_s, fwd_r, trade_s, trade_r, mate_s, mate_r, back_s, back_r,
):
    me = lax.axis_index("dev")
    chip, core = lax.div(me, 2), lax.rem(me, 2)
    cx, cz = lax.div(chip, 4), lax.rem(chip, 4)
    other_core = 1 - core
    mate = chip * 2 + other_core
    partner = lax.rem(me + 16, 32)
    xs = [cx] + [lax.rem(cx + d, 4) for d in (1, 2, 3)]
    zs = [cz] + [lax.rem(cz + d, 4) for d in (1, 2, 3)]
    away = [(dx, dz) for dx in (2, 1, 3, 0) for dz in (2, 1, 3, 0) if (dx, dz) != (0, 0)]
    to = [(xs[dx] * 4 + zs[dz]) * 2 + core for dx, dz in away]
    source = [(xs[(4 - dx) % 4] * 4 + zs[(4 - dz) % 4]) * 2 + core for dx, dz in away]

    loads = [
        pltpu.make_async_copy(tok_hbm, tok, small_sem.at[0]),
        pltpu.make_async_copy(rout_hbm, rout, small_sem.at[1]),
        pltpu.make_async_copy(gw_hbm, gw, small_sem.at[2]),
        pltpu.make_async_copy(trade_hbm, trade_slot, small_sem.at[3]),
        pltpu.make_async_copy(len_hbm, lengths, small_sem.at[4]),
        pltpu.make_async_copy(q_hbm, q, q_sem),
        pltpu.make_async_copy(k_hbm, k, k_sem),
    ]
    tok_load, rout_load, gw_load, trade_load, len_load, q_load, k_load = loads
    wg_loads, wu_loads, wd_loads = [], [], []
    for i, (first, last) in enumerate(CUTS):
        rows = pl.ds(first * W, (last - first) * W)
        wg_loads.append(pltpu.make_async_copy(wg_hbm.at[0, rows], wg.at[rows], wg_sem.at[i]))
        wu_loads.append(pltpu.make_async_copy(wu_hbm.at[0, rows], wu.at[rows], wu_sem.at[i]))
        wd_loads.append(
            pltpu.make_async_copy(wd_hbm.at[0, :, rows], wd.at[:, rows], wd_sem.at[i])
        )
    for load in loads[:3]:
        load.start()
    barrier = pltpu.get_barrier_semaphore()
    for other in to + [mate]:
        pl.semaphore_signal(barrier, inc=1, device_id={"dev": other}, device_id_type=MESH)
    for load in loads[3:]:
        load.start()

    row = lax.broadcasted_iota(jnp.int32, (256, 256), 0)
    col = lax.broadcasted_iota(jnp.int32, (256, 256), 1)
    perm[0] = jnp.where(col == (row % 32) * SLOTS + row // 32, 1.0, 0.0).astype(bf16)
    perm[1] = jnp.where(row == (col % 32) * SLOTS + col // 32, 1.0, 0.0).astype(bf16)

    tok_load.wait()
    rout_load.wait()
    gw_load.wait()
    tokens = tok[...].astype(f32)
    lane = lax.broadcasted_iota(jnp.int32, (2, W), 1)
    factor = jnp.zeros((2, W), f32)
    for top in range(8):
        expert, weight = rout[:, top : top + 1], gw[:, top : top + 1]
        hit = (lane == expert) | (lane == expert + 32)
        factor = factor + jnp.where(hit, weight, 0.0)
    high = factor.astype(bf16).astype(f32)
    factor = jnp.where(lane < 32, high, factor - high)
    for t in range(2):
        for s in range(PIECES):
            stage[t * SLOTS + s : t * SLOTS + s + 1, :] = tokens[t : t + 1, s * W : (s + 1) * W]
        stage[t * SLOTS + PIECES : (t + 1) * SLOTS, :] = factor[t : t + 1]
    gathered[core, 15] = stage[...].astype(bf16)
    for i in range(2):
        wg_loads[i].start()
        wu_loads[i].start()

    pl.semaphore_wait(barrier, 16)

    own = gathered.at[core, 15]
    tok_copies = [
        send(own, gathered.at[core, i], tok_s.at[i], tok_r.at[i], to[i]) for i in range(15)
    ]
    for copy in tok_copies:
        copy.start()

    trade_load.wait()
    len_load.wait()
    trade_at = trade_slot[me % 16]
    keep_at = 1 - trade_at
    q_load.wait()
    q_out[...] = q[trade_at]
    q_copy = send(q_out, q_in, trade_s.at[0], trade_r.at[0], partner)

    k_load.wait()
    kept = attend(q[keep_at], k[keep_at], lengths[me * 2 + keep_at])
    q_copy.start()
    for i in range(2):
        wd_loads[i].start()

    def spread(side):
        rows = jnp.dot(
            perm[0], gathered[side].reshape(256, W), preferred_element_type=f32
        )
        for s in range(PIECES):
            tok_rows[s, side] = rows[s * 32 : (s + 1) * 32].astype(bf16)
        factors[side] = rows[PIECES * 32 :]

    fwd_copies = []
    for i, (first, last) in enumerate(BATCHES):
        for copy in tok_copies[first : min(last, 15)]:
            copy.wait_recv()
        batch = gathered.at[core, pl.ds(first, last - first)]
        fwd_copies.append(send(batch, batch, fwd_s.at[i], fwd_r.at[i], mate))
        fwd_copies[i].start()
    spread(core)
    for copy in fwd_copies:
        copy.wait_recv()
    spread(other_core)

    gate = jnp.zeros((64, 1024), f32)
    up = jnp.zeros((64, 1024), f32)
    for i, (first, last) in enumerate(CUTS):
        wg_loads[i].wait()
        wu_loads[i].wait()
        for s in range(first, last):
            x = tok_rows[s].reshape(64, W)
            rows = slice(s * W, (s + 1) * W)
            gate += jnp.dot(x, wg[rows, :], preferred_element_type=f32)
            up += jnp.dot(x, wu[rows, :], preferred_element_type=f32)
    hidden = (gate / (1.0 + jnp.exp(-gate)) * up).astype(bf16)
    lane = lax.broadcasted_iota(jnp.int32, (64, W), 1)
    mine = (lane == me) | (lane == me + 32)
    weight = jnp.sum(jnp.where(mine, factors[...].reshape(64, W), 0.0), axis=1, keepdims=True)

    q_copy.wait_recv()
    o_out[...] = attend(q_in[...], k[trade_at], lengths[me * 2 + trade_at])
    o_copy = send(o_out, o_in, trade_s.at[1], trade_r.at[1], partner)
    o_copy.start()

    mate_copies = []
    for i, (first, last) in enumerate(CUTS):
        wd_loads[i].wait()
        for s in range(first, last):
            y = jnp.dot(hidden, wd[:, s * W : (s + 1) * W], preferred_element_type=f32)
            y = (y.astype(bf16).astype(f32) * weight).astype(bf16)
            sums[0, s] = y[:32]
            sums[1, s] = y[32:]
        cut = pl.ds(first, last - first)
        mate_copies.append(
            send(sums.at[other_core, cut], mate_in.at[cut], mate_s.at[i], mate_r.at[i], mate)
        )
        mate_copies[i].start()
    for copy in mate_copies:
        copy.wait_recv()
    part = (sums[core].astype(f32) + mate_in[...].astype(f32)).astype(bf16)
    part = jnp.concatenate([part.reshape(PIECES * 32, W), jnp.zeros((32, W), bf16)], axis=0)
    back[...] = (
        jnp.dot(perm[1], part, preferred_element_type=f32).astype(bf16).reshape(16, 16, W)
    )
    back_copies = [
        send(back.at[i], landed.at[i], back_s.at[i], back_r.at[i], source[i])
        for i in range(15)
    ]
    for copy in back_copies:
        copy.start()

    for copy in tok_copies + mate_copies + fwd_copies + [q_copy, o_copy]:
        copy.wait_send()
    o_copy.wait_recv()
    arrived = o_in[...]
    att[0] = jnp.where(trade_at == 0, arrived, kept)
    att[1] = jnp.where(trade_at == 1, arrived, kept)

    for copy in back_copies:
        copy.wait_recv()
    total = back[15].astype(f32)
    for i in range(15):
        total += landed[i].astype(f32)
    exp_ref[...] = total.astype(bf16)
    for copy in back_copies:
        copy.wait_send()


def finish(att_ref, row_ref, att_hbm, exp_hbm, line, exp, sem):
    att_copy = pltpu.make_async_copy(att_ref, att_hbm, sem.at[0])
    att_copy.start()
    rows = row_ref[...].astype(f32)
    for t in range(2):
        for s in range(PIECES):
            line[t : t + 1, s * W : (s + 1) * W] = rows[t * SLOTS + s : t * SLOTS + s + 1]
    exp[...] = line[...].astype(bf16)
    exp_copy = pltpu.make_async_copy(exp, exp_hbm, sem.at[1])
    exp_copy.start()
    att_copy.wait()
    exp_copy.wait()


def local(
    queries, latent_cache, lengths, trade_slot, tokens, routing, gate_weights, w_gate, w_up, w_down
):
    hbm_spec = pl.BlockSpec(memory_space=pltpu.HBM)
    dma = pltpu.SemaphoreType.DMA
    vmem = pltpu.VMEM
    attended, rows = pl.pallas_call(
        kernel,
        out_shape=(
            pltpu.VMEM((2, 128, LAT), bf16),
            pltpu.VMEM((16, W), bf16),
        ),
        in_specs=[hbm_spec] * 10,
        out_specs=(pl.BlockSpec(memory_space=pltpu.VMEM),) * 2,
        scratch_shapes=[
            pltpu.SMEM((64,), jnp.int32),
            pltpu.SMEM((16,), jnp.int32),
            vmem((2, 3584), bf16),
            vmem((2, 8), jnp.int32),
            vmem((2, 8), f32),
            vmem((2, 576, 128), bf16),
            vmem((2, 576, 1024), bf16),
            vmem((3584, 1024), bf16),
            vmem((3584, 1024), bf16),
            vmem((1024, 3584), bf16),
            vmem((16, W), f32),
            vmem((2, 256, 256), bf16),
            vmem((2, 16, 16, W), bf16),
            vmem((PIECES, 2, 32, W), bf16),
            vmem((2, 32, W), f32),
            vmem((576, 128), bf16),
            vmem((576, 128), bf16),
            vmem((128, LAT), bf16),
            vmem((128, LAT), bf16),
            vmem((2, PIECES, 32, W), bf16),
            vmem((PIECES, 32, W), bf16),
            vmem((16, 16, W), bf16),
            vmem((15, 16, W), bf16),
            dma((5,)),
            dma,
            dma,
            dma((2,)),
            dma((2,)),
            dma((2,)),
            dma((15,)),
            dma((15,)),
            dma((2,)),
            dma((2,)),
            dma((2,)),
            dma((2,)),
            dma((2,)),
            dma((2,)),
            dma((15,)),
            dma((15,)),
        ],
        compiler_params=pltpu.CompilerParams(
            collective_id=0, has_side_effects=True, vmem_limit_bytes=56 * 2**20
        ),
        cost_estimate=pl.CostEstimate(
            flops=2_000_000_000, bytes_accessed=25_000_000, transcendentals=400_000
        ),
    )(
        *[
            pltpu.with_memory_space_constraint(operand, pltpu.HBM)
            for operand in (
                jnp.swapaxes(queries, 1, 2),
                jnp.swapaxes(latent_cache, 1, 2),
                lengths,
                trade_slot,
                tokens,
                routing,
                gate_weights,
                w_gate,
                w_up,
                w_down,
            )
        ]
    )
    return pl.pallas_call(
        finish,
        out_shape=(pltpu.HBM((2, 128, LAT), bf16), pltpu.HBM((2, PIECES * W), bf16)),
        in_specs=[pl.BlockSpec(memory_space=pltpu.VMEM)] * 2,
        out_specs=(hbm_spec,) * 2,
        scratch_shapes=[vmem((2, PIECES * W), f32), vmem((2, PIECES * W), bf16), dma((2,))],
    )(
        pltpu.with_memory_space_constraint(attended, pltpu.VMEM),
        pltpu.with_memory_space_constraint(rows, pltpu.VMEM),
    )


def solution(mesh):
    in_specs = (
        P(("rep", "dev"), None, None),
        P(("rep", "dev"), None, None),
        P("rep"),
        P("rep"),
        P(("rep", "dev"), None),
        P(("rep", "dev"), None),
        P(("rep", "dev"), None),
        P("dev", None, None),
        P("dev", None, None),
        P("dev", None, None),
    )
    out_specs = (P(("rep", "dev"), None, None), P(("rep", "dev"), None))
    return jax.shard_map(local, mesh=mesh, in_specs=in_specs, out_specs=out_specs, check_vma=False)
```

```python
import functools

import jax
import jax.numpy as jnp
from jax import lax
from jax.experimental import pallas as pl
from jax.experimental.pallas import tpu as pltpu
from jax.sharding import PartitionSpec as P

LAT = 512
W = 512
CUTS = ((0, 4), (4, 7))
BATCHES = ((0, 16),)
PIECES = 7
SLOTS = 8
score_scale = 192.0 ** (-0.5)
MESH = pl.DeviceIdType.MESH
f32 = jnp.float32
bf16 = jnp.bfloat16


def send(src, dst, send_sem, recv_sem, to):
    return pltpu.make_async_remote_copy(
        src_ref=src,
        dst_ref=dst,
        send_sem=send_sem,
        recv_sem=recv_sem,
        device_id={"dev": to},
        device_id_type=MESH,
    )


def all_fifteen(blocks, sem):
    pltpu.make_async_copy(blocks, blocks, sem).wait()


def attend(q_t, k_t, live):
    scores = (
        lax.dot_general(q_t, k_t, (((0,), (0,)), ((), ())), preferred_element_type=f32)
        * score_scale
    )
    position = lax.broadcasted_iota(jnp.int32, scores.shape, 1)
    scores = jnp.where(position < live, scores, -jnp.inf)
    weights = jnp.exp(scores - jnp.max(scores, axis=1, keepdims=True))
    shares = (weights / jnp.sum(weights, axis=1, keepdims=True)).astype(bf16)
    return lax.dot_general(
        shares, k_t[:LAT], (((1,), (1,)), ((), ())), preferred_element_type=f32
    ).astype(bf16)


def kernel(
    q_hbm, k_hbm, len_hbm, trade_hbm, tok_hbm, rout_hbm, gw_hbm, wg_hbm, wu_hbm, wd_hbm,
    att, exp_ref,
    lengths, trade_slot, tok, rout, gw, q, k, wg, wu, wd, stage, perm, gathered, tok_rows, factors,
    q_out, q_in, o_out, o_in, sums, mate_in, back, landed,
    small_sem, q_sem, k_sem, wg_sem, wu_sem, wd_sem,
    tok_s, tok_r, fwd_s, fwd_r, trade_s, trade_r, mate_s, mate_r, back_s, back_r,
):
    me = lax.axis_index("dev")
    chip, core = lax.div(me, 2), lax.rem(me, 2)
    cx, cz = lax.div(chip, 4), lax.rem(chip, 4)
    other_core = 1 - core
    mate = chip * 2 + other_core
    partner = lax.rem(me + 16, 32)
    xs = [cx] + [lax.rem(cx + d, 4) for d in (1, 2, 3)]
    zs = [cz] + [lax.rem(cz + d, 4) for d in (1, 2, 3)]
    away = [(dx, dz) for dx in (2, 1, 3, 0) for dz in (2, 1, 3, 0) if (dx, dz) != (0, 0)]
    to = [(xs[dx] * 4 + zs[dz]) * 2 + core for dx, dz in away]
    source = [(xs[(4 - dx) % 4] * 4 + zs[(4 - dz) % 4]) * 2 + core for dx, dz in away]

    loads = [
        pltpu.make_async_copy(tok_hbm, tok, small_sem.at[0]),
        pltpu.make_async_copy(rout_hbm, rout, small_sem.at[1]),
        pltpu.make_async_copy(gw_hbm, gw, small_sem.at[2]),
        pltpu.make_async_copy(trade_hbm, trade_slot, small_sem.at[3]),
        pltpu.make_async_copy(len_hbm, lengths, small_sem.at[4]),
        pltpu.make_async_copy(q_hbm, q, q_sem),
        pltpu.make_async_copy(k_hbm, k, k_sem),
    ]
    tok_load, rout_load, gw_load, trade_load, len_load, q_load, k_load = loads
    wg_loads, wu_loads, wd_loads = [], [], []
    for i, (first, last) in enumerate(CUTS):
        rows = pl.ds(first * W, (last - first) * W)
        wg_loads.append(pltpu.make_async_copy(wg_hbm.at[0, rows], wg.at[rows], wg_sem.at[i]))
        wu_loads.append(pltpu.make_async_copy(wu_hbm.at[0, rows], wu.at[rows], wu_sem.at[i]))
        wd_loads.append(
            pltpu.make_async_copy(wd_hbm.at[0, :, rows], wd.at[:, rows], wd_sem.at[i])
        )
    for load in loads[:3]:
        load.start()
    barrier = pltpu.get_barrier_semaphore()
    for other in to + [mate]:
        pl.semaphore_signal(barrier, inc=1, device_id={"dev": other}, device_id_type=MESH)
    for load in loads[3:]:
        load.start()

    tok_rows[:, 2:] = jnp.zeros((PIECES, 2, 32, W), bf16)
    row = lax.broadcasted_iota(jnp.int32, (256, 256), 0)
    col = lax.broadcasted_iota(jnp.int32, (256, 256), 1)
    perm[0] = jnp.where(col == (row % 32) * SLOTS + row // 32, 1.0, 0.0).astype(bf16)
    perm[1] = jnp.where(row == (col % 32) * SLOTS + col // 32, 1.0, 0.0).astype(bf16)

    tok_load.wait()
    rout_load.wait()
    gw_load.wait()
    tokens = tok[...].astype(f32)
    lane = lax.broadcasted_iota(jnp.int32, (2, W), 1)
    factor = jnp.zeros((2, W), f32)
    for top in range(8):
        expert, weight = rout[:, top : top + 1], gw[:, top : top + 1]
        hit = (lane == expert) | (lane == expert + 32)
        factor = factor + jnp.where(hit, weight, 0.0)
    high = factor.astype(bf16).astype(f32)
    factor = jnp.where(lane < 32, high, factor - high)
    for t in range(2):
        for s in range(PIECES):
            stage[t * SLOTS + s : t * SLOTS + s + 1, :] = tokens[t : t + 1, s * W : (s + 1) * W]
        stage[t * SLOTS + PIECES : (t + 1) * SLOTS, :] = factor[t : t + 1]
    gathered[core, 15] = stage[...].astype(bf16)
    for i in range(2):
        wg_loads[i].start()
        wu_loads[i].start()

    pl.semaphore_wait(barrier, 16)

    own = gathered.at[core, 15]
    tok_copies = [
        send(own, gathered.at[core, i], tok_s, tok_r, to[i]) for i in range(15)
    ]
    for copy in tok_copies:
        copy.start()

    trade_load.wait()
    len_load.wait()
    trade_at = trade_slot[me % 16]
    keep_at = 1 - trade_at
    q_load.wait()
    q_out[...] = q[trade_at]
    q_copy = send(q_out, q_in, trade_s.at[0], trade_r.at[0], partner)

    k_load.wait()
    kept = attend(q[keep_at], k[keep_at], lengths[me * 2 + keep_at])
    q_copy.start()
    for i in range(2):
        wd_loads[i].start()

    def spread(side):
        rows = jnp.dot(
            perm[0], gathered[side].reshape(256, W), preferred_element_type=f32
        )
        for s in range(PIECES):
            tok_rows[s, side] = rows[s * 32 : (s + 1) * 32].astype(bf16)
        factors[side] = rows[PIECES * 32 :]

    fwd_copies = []
    for i, (first, last) in enumerate(BATCHES):
        all_fifteen(gathered.at[core, pl.ds(0, 15)], tok_r)
        batch = gathered.at[core, pl.ds(first, last - first)]
        fwd_copies.append(send(batch, batch, fwd_s.at[i], fwd_r.at[i], mate))
        fwd_copies[i].start()
    spread(core)
    for copy in fwd_copies:
        copy.wait_recv()
    spread(other_core)

    gate = jnp.zeros((128, 1024), f32)
    up = jnp.zeros((128, 1024), f32)
    for i, (first, last) in enumerate(CUTS):
        wg_loads[i].wait()
        wu_loads[i].wait()
        for s in range(first, last):
            x = tok_rows[s].reshape(128, W)
            rows = slice(s * W, (s + 1) * W)
            gate += jnp.dot(x, wg[rows, :], preferred_element_type=f32)
            up += jnp.dot(x, wu[rows, :], preferred_element_type=f32)
    gate, up = gate[:64], up[:64]
    hidden = (gate / (1.0 + jnp.exp(-gate)) * up).astype(bf16)
    hidden = jnp.concatenate([hidden, jnp.zeros((64, 1024), bf16)], axis=0)
    lane = lax.broadcasted_iota(jnp.int32, (64, W), 1)
    mine = (lane == me) | (lane == me + 32)
    weight = jnp.sum(jnp.where(mine, factors[...].reshape(64, W), 0.0), axis=1, keepdims=True)

    q_copy.wait_recv()
    o_out[...] = attend(q_in[...], k[trade_at], lengths[me * 2 + trade_at])
    o_copy = send(o_out, o_in, trade_s.at[1], trade_r.at[1], partner)
    o_copy.start()

    mate_copies = []
    for i, (first, last) in enumerate(CUTS):
        wd_loads[i].wait()
        for s in range(first, last):
            y = jnp.dot(hidden, wd[:, s * W : (s + 1) * W], preferred_element_type=f32)[:64]
            y = (y.astype(bf16).astype(f32) * weight).astype(bf16)
            sums[0, s] = y[:32]
            sums[1, s] = y[32:]
        cut = pl.ds(first, last - first)
        mate_copies.append(
            send(sums.at[other_core, cut], mate_in.at[cut], mate_s.at[i], mate_r.at[i], mate)
        )
        mate_copies[i].start()
    for copy in mate_copies:
        copy.wait_recv()
    part = (sums[core].astype(f32) + mate_in[...].astype(f32)).astype(bf16)
    part = jnp.concatenate([part.reshape(PIECES * 32, W), jnp.zeros((32, W), bf16)], axis=0)
    back[...] = (
        jnp.dot(perm[1], part, preferred_element_type=f32).astype(bf16).reshape(16, 16, W)
    )
    back_copies = [
        send(back.at[i], landed.at[i], back_s, back_r, source[i])
        for i in range(15)
    ]
    for copy in back_copies:
        copy.start()

    all_fifteen(gathered.at[core, pl.ds(0, 15)], tok_s)
    for copy in mate_copies + fwd_copies + [q_copy, o_copy]:
        copy.wait_send()
    o_copy.wait_recv()
    arrived = o_in[...]
    att[0] = jnp.where(trade_at == 0, arrived, kept)
    att[1] = jnp.where(trade_at == 1, arrived, kept)

    all_fifteen(landed, back_r)
    total = back[15].astype(f32)
    for i in range(15):
        total += landed[i].astype(f32)
    exp_ref[...] = total.astype(bf16)
    all_fifteen(landed, back_s)


def finish(att_ref, row_ref, att_hbm, exp_hbm, line, exp, sem):
    att_copy = pltpu.make_async_copy(att_ref, att_hbm, sem.at[0])
    att_copy.start()
    rows = row_ref[...].astype(f32)
    for t in range(2):
        for s in range(PIECES):
            line[t : t + 1, s * W : (s + 1) * W] = rows[t * SLOTS + s : t * SLOTS + s + 1]
    exp[...] = line[...].astype(bf16)
    exp_copy = pltpu.make_async_copy(exp, exp_hbm, sem.at[1])
    exp_copy.start()
    att_copy.wait()
    exp_copy.wait()


def local(
    queries, latent_cache, lengths, trade_slot, tokens, routing, gate_weights, w_gate, w_up, w_down
):
    hbm_spec = pl.BlockSpec(memory_space=pltpu.HBM)
    dma = pltpu.SemaphoreType.DMA
    vmem = pltpu.VMEM
    attended, rows = pl.pallas_call(
        kernel,
        out_shape=(
            pltpu.VMEM((2, 128, LAT), bf16),
            pltpu.VMEM((16, W), bf16),
        ),
        in_specs=[hbm_spec] * 10,
        out_specs=(pl.BlockSpec(memory_space=pltpu.VMEM),) * 2,
        scratch_shapes=[
            pltpu.SMEM((64,), jnp.int32),
            pltpu.SMEM((16,), jnp.int32),
            vmem((2, 3584), bf16),
            vmem((2, 8), jnp.int32),
            vmem((2, 8), f32),
            vmem((2, 576, 128), bf16),
            vmem((2, 576, 1024), bf16),
            vmem((3584, 1024), bf16),
            vmem((3584, 1024), bf16),
            vmem((1024, 3584), bf16),
            vmem((16, W), f32),
            vmem((2, 256, 256), bf16),
            vmem((2, 16, 16, W), bf16),
            vmem((PIECES, 4, 32, W), bf16),
            vmem((2, 32, W), f32),
            vmem((576, 128), bf16),
            vmem((576, 128), bf16),
            vmem((128, LAT), bf16),
            vmem((128, LAT), bf16),
            vmem((2, PIECES, 32, W), bf16),
            vmem((PIECES, 32, W), bf16),
            vmem((16, 16, W), bf16),
            vmem((15, 16, W), bf16),
            dma((5,)),
            dma,
            dma,
            dma((2,)),
            dma((2,)),
            dma((2,)),
            dma,
            dma,
            dma((2,)),
            dma((2,)),
            dma((2,)),
            dma((2,)),
            dma((2,)),
            dma((2,)),
            dma,
            dma,
        ],
        compiler_params=pltpu.CompilerParams(
            collective_id=0, has_side_effects=True, vmem_limit_bytes=56 * 2**20
        ),
        cost_estimate=pl.CostEstimate(
            flops=2_000_000_000, bytes_accessed=25_000_000, transcendentals=400_000
        ),
    )(
        *[
            pltpu.with_memory_space_constraint(operand, pltpu.HBM)
            for operand in (
                jnp.swapaxes(queries, 1, 2),
                jnp.swapaxes(latent_cache, 1, 2),
                lengths,
                trade_slot,
                tokens,
                routing,
                gate_weights,
                w_gate,
                w_up,
                w_down,
            )
        ]
    )
    return pl.pallas_call(
        finish,
        out_shape=(pltpu.HBM((2, 128, LAT), bf16), pltpu.HBM((2, PIECES * W), bf16)),
        in_specs=[pl.BlockSpec(memory_space=pltpu.VMEM)] * 2,
        out_specs=(hbm_spec,) * 2,
        scratch_shapes=[vmem((2, PIECES * W), f32), vmem((2, PIECES * W), bf16), dma((2,))],
    )(
        pltpu.with_memory_space_constraint(attended, pltpu.VMEM),
        pltpu.with_memory_space_constraint(rows, pltpu.VMEM),
    )


def solution(mesh):
    in_specs = (
        P(("rep", "dev"), None, None),
        P(("rep", "dev"), None, None),
        P("rep"),
        P("rep"),
        P(("rep", "dev"), None),
        P(("rep", "dev"), None),
        P(("rep", "dev"), None),
        P("dev", None, None),
        P("dev", None, None),
        P("dev", None, None),
    )
    out_specs = (P(("rep", "dev"), None, None), P(("rep", "dev"), None))
    return jax.shard_map(local, mesh=mesh, in_specs=in_specs, out_specs=out_specs, check_vma=False)
```

```python
import functools

import jax
import jax.numpy as jnp
from jax import lax
from jax.experimental import pallas as pl
from jax.experimental.pallas import tpu as pltpu
from jax.sharding import PartitionSpec as P

LAT = 512
W = 512
CUTS = ((0, 4), (4, 7))
BATCHES = ((0, 16),)
PIECES = 7
SLOTS = 8
score_scale = 192.0 ** (-0.5)
MESH = pl.DeviceIdType.MESH
f32 = jnp.float32
bf16 = jnp.bfloat16


def send(src, dst, send_sem, recv_sem, to):
    return pltpu.make_async_remote_copy(
        src_ref=src,
        dst_ref=dst,
        send_sem=send_sem,
        recv_sem=recv_sem,
        device_id={"dev": to},
        device_id_type=MESH,
    )


def all_fifteen(blocks, sem):
    pltpu.make_async_copy(blocks, blocks, sem).wait()


def attend(q_t, k_t, live):
    scores = (
        lax.dot_general(q_t, k_t, (((0,), (0,)), ((), ())), preferred_element_type=f32)
        * score_scale
    )
    position = lax.broadcasted_iota(jnp.int32, scores.shape, 1)
    scores = jnp.where(position < live, scores, -jnp.inf)
    weights = jnp.exp(scores - jnp.max(scores, axis=1, keepdims=True))
    shares = (weights / jnp.sum(weights, axis=1, keepdims=True)).astype(bf16)
    return lax.dot_general(
        shares, k_t[:LAT], (((1,), (1,)), ((), ())), preferred_element_type=f32
    ).astype(bf16)


def kernel(
    q_hbm, k_hbm, len_hbm, trade_hbm, tok_hbm, rout_hbm, gw_hbm, wg_hbm, wu_hbm, wd_hbm,
    att, exp_ref,
    lengths, trade_slot, tok, rout, gw, q, k, wg, wu, wd, stage, perm, gathered, tok_rows, factors,
    q_out, q_in, o_out, o_in, sums, mate_in, back, landed,
    small_sem, q_sem, k_sem, wg_sem, wu_sem, wd_sem,
    tok_s, tok_r, fwd_s, fwd_r, trade_s, trade_r, mate_s, mate_r, back_s, back_r,
):
    me = lax.axis_index("dev")
    chip, core = lax.div(me, 2), lax.rem(me, 2)
    cx, cz = lax.div(chip, 4), lax.rem(chip, 4)
    other_core = 1 - core
    mate = chip * 2 + other_core
    partner = lax.rem(me + 16, 32)
    xs = [cx] + [lax.rem(cx + d, 4) for d in (1, 2, 3)]
    zs = [cz] + [lax.rem(cz + d, 4) for d in (1, 2, 3)]
    away = [(2, 2), (2, 1), (1, 2), (2, 3), (3, 2), (2, 0), (0, 2), (1, 1), (3, 3), (1, 3), (3, 1)]
    away += [(1, 0), (0, 1), (3, 0), (0, 3)]
    to = [(xs[dx] * 4 + zs[dz]) * 2 + core for dx, dz in away]
    source = [(xs[(4 - dx) % 4] * 4 + zs[(4 - dz) % 4]) * 2 + core for dx, dz in away]

    loads = [
        pltpu.make_async_copy(tok_hbm, tok, small_sem.at[0]),
        pltpu.make_async_copy(rout_hbm, rout, small_sem.at[1]),
        pltpu.make_async_copy(gw_hbm, gw, small_sem.at[2]),
        pltpu.make_async_copy(trade_hbm, trade_slot, small_sem.at[3]),
        pltpu.make_async_copy(len_hbm, lengths, small_sem.at[4]),
        pltpu.make_async_copy(q_hbm, q, q_sem),
        pltpu.make_async_copy(k_hbm, k, k_sem),
    ]
    tok_load, rout_load, gw_load, trade_load, len_load, q_load, k_load = loads
    wg_loads, wu_loads, wd_loads = [], [], []
    for i, (first, last) in enumerate(CUTS):
        rows = pl.ds(first * W, (last - first) * W)
        wg_loads.append(pltpu.make_async_copy(wg_hbm.at[0, rows], wg.at[rows], wg_sem.at[i]))
        wu_loads.append(pltpu.make_async_copy(wu_hbm.at[0, rows], wu.at[rows], wu_sem.at[i]))
        wd_loads.append(
            pltpu.make_async_copy(wd_hbm.at[0, :, rows], wd.at[:, rows], wd_sem.at[i])
        )
    for load in loads[:3]:
        load.start()
    barrier = pltpu.get_barrier_semaphore()
    for other in to + [mate]:
        pl.semaphore_signal(barrier, inc=1, device_id={"dev": other}, device_id_type=MESH)
    for load in loads[3:]:
        load.start()

    tok_load.wait()
    rout_load.wait()
    gw_load.wait()
    tokens = tok[...].astype(f32)
    lane = lax.broadcasted_iota(jnp.int32, (2, W), 1)
    factor = jnp.zeros((2, W), f32)
    for top in range(8):
        expert, weight = rout[:, top : top + 1], gw[:, top : top + 1]
        hit = (lane == expert) | (lane == expert + 32)
        factor = factor + jnp.where(hit, weight, 0.0)
    high = factor.astype(bf16).astype(f32)
    factor = jnp.where(lane < 32, high, factor - high)
    for t in range(2):
        for s in range(PIECES):
            stage[t * SLOTS + s : t * SLOTS + s + 1, :] = tokens[t : t + 1, s * W : (s + 1) * W]
        stage[t * SLOTS + PIECES : (t + 1) * SLOTS, :] = factor[t : t + 1]
    gathered[core, 15] = stage[...].astype(bf16)
    for i in range(2):
        wg_loads[i].start()
        wu_loads[i].start()

    pl.semaphore_wait(barrier, 16)

    own = gathered.at[core, 15]
    tok_copies = [
        send(own, gathered.at[core, i], tok_s, tok_r, to[i]) for i in range(15)
    ]
    for copy in tok_copies:
        copy.start()

    tok_rows[:, 2:] = jnp.zeros((PIECES, 2, 32, W), bf16)
    row = lax.broadcasted_iota(jnp.int32, (256, 256), 0)
    col = lax.broadcasted_iota(jnp.int32, (256, 256), 1)
    perm[0] = jnp.where(col == (row & 31) * SLOTS + (row >> 5), 1.0, 0.0).astype(bf16)
    perm[1] = jnp.where(row == (col & 31) * SLOTS + (col >> 5), 1.0, 0.0).astype(bf16)

    trade_load.wait()
    len_load.wait()
    trade_at = trade_slot[me % 16]
    keep_at = 1 - trade_at
    q_load.wait()
    q_out[...] = q[trade_at]
    q_copy = send(q_out, q_in, trade_s.at[0], trade_r.at[0], partner)
    q_copy.start()

    k_load.wait()
    kept = attend(q[keep_at], k[keep_at], lengths[me * 2 + keep_at])
    for i in range(2):
        wd_loads[i].start()

    def spread(side):
        rows = jnp.dot(
            perm[0], gathered[side].reshape(256, W), preferred_element_type=f32
        )
        for s in range(PIECES):
            tok_rows[s, side] = rows[s * 32 : (s + 1) * 32].astype(bf16)
        factors[side] = rows[PIECES * 32 :]

    fwd_copies = []
    for i, (first, last) in enumerate(BATCHES):
        all_fifteen(gathered.at[core, pl.ds(0, 15)], tok_r)
        batch = gathered.at[core, pl.ds(first, last - first)]
        fwd_copies.append(send(batch, batch, fwd_s.at[i], fwd_r.at[i], mate))
        fwd_copies[i].start()
    spread(core)
    for copy in fwd_copies:
        copy.wait_recv()
    spread(other_core)

    gate = jnp.zeros((128, 1024), f32)
    up = jnp.zeros((128, 1024), f32)
    for i, (first, last) in enumerate(CUTS):
        if i == 1:
            q_copy.wait_recv()
            o_out[...] = attend(q_in[...], k[trade_at], lengths[me * 2 + trade_at])
            o_copy = send(o_out, o_in, trade_s.at[1], trade_r.at[1], partner)
            o_copy.start()
        wg_loads[i].wait()
        wu_loads[i].wait()
        for s in range(first, last):
            x = tok_rows[s].reshape(128, W)
            rows = slice(s * W, (s + 1) * W)
            gate += jnp.dot(x, wg[rows, :], preferred_element_type=f32)
            up += jnp.dot(x, wu[rows, :], preferred_element_type=f32)
    gate, up = gate[:64], up[:64]
    hidden = (gate / (1.0 + jnp.exp(-gate)) * up).astype(bf16)
    hidden = jnp.concatenate([hidden, jnp.zeros((64, 1024), bf16)], axis=0)
    lane = lax.broadcasted_iota(jnp.int32, (64, W), 1)
    mine = (lane == me) | (lane == me + 32)
    weight = jnp.sum(jnp.where(mine, factors[...].reshape(64, W), 0.0), axis=1, keepdims=True)

    mate_copies = []
    for i, (first, last) in enumerate(CUTS):
        wd_loads[i].wait()
        for s in range(first, last):
            y = jnp.dot(hidden, wd[:, s * W : (s + 1) * W], preferred_element_type=f32)[:64]
            y = (y.astype(bf16).astype(f32) * weight).astype(bf16)
            sums[0, s] = y[:32]
            sums[1, s] = y[32:]
        cut = pl.ds(first, last - first)
        mate_copies.append(
            send(sums.at[other_core, cut], mate_in.at[cut], mate_s.at[i], mate_r.at[i], mate)
        )
        mate_copies[i].start()
    for copy in mate_copies:
        copy.wait_recv()
    part = (sums[core].astype(f32) + mate_in[...].astype(f32)).astype(bf16)
    part = jnp.concatenate([part.reshape(PIECES * 32, W), jnp.zeros((32, W), bf16)], axis=0)
    back[...] = (
        jnp.dot(perm[1], part, preferred_element_type=f32).astype(bf16).reshape(16, 16, W)
    )
    back_copies = [
        send(back.at[i], landed.at[i], back_s, back_r, source[i])
        for i in range(15)
    ]
    for copy in back_copies:
        copy.start()

    all_fifteen(gathered.at[core, pl.ds(0, 15)], tok_s)
    for copy in mate_copies + fwd_copies + [q_copy, o_copy]:
        copy.wait_send()
    o_copy.wait_recv()
    arrived = o_in[...]
    att[0] = jnp.where(trade_at == 0, arrived, kept)
    att[1] = jnp.where(trade_at == 1, arrived, kept)

    all_fifteen(landed, back_r)
    total = back[15].astype(f32)
    for i in range(15):
        total += landed[i].astype(f32)
    exp_ref[...] = total.astype(bf16)
    all_fifteen(landed, back_s)


def finish(att_ref, row_ref, att_hbm, exp_hbm, line, exp, sem):
    att_copy = pltpu.make_async_copy(att_ref, att_hbm, sem.at[0])
    att_copy.start()
    rows = row_ref[...].astype(f32)
    for t in range(2):
        for s in range(PIECES):
            line[t : t + 1, s * W : (s + 1) * W] = rows[t * SLOTS + s : t * SLOTS + s + 1]
    exp[...] = line[...].astype(bf16)
    exp_copy = pltpu.make_async_copy(exp, exp_hbm, sem.at[1])
    exp_copy.start()
    att_copy.wait()
    exp_copy.wait()


def local(
    queries, latent_cache, lengths, trade_slot, tokens, routing, gate_weights, w_gate, w_up, w_down
):
    hbm_spec = pl.BlockSpec(memory_space=pltpu.HBM)
    dma = pltpu.SemaphoreType.DMA
    vmem = pltpu.VMEM
    attended, rows = pl.pallas_call(
        kernel,
        out_shape=(
            pltpu.VMEM((2, 128, LAT), bf16),
            pltpu.VMEM((16, W), bf16),
        ),
        in_specs=[hbm_spec] * 10,
        out_specs=(pl.BlockSpec(memory_space=pltpu.VMEM),) * 2,
        scratch_shapes=[
            pltpu.SMEM((64,), jnp.int32),
            pltpu.SMEM((16,), jnp.int32),
            vmem((2, 3584), bf16),
            vmem((2, 8), jnp.int32),
            vmem((2, 8), f32),
            vmem((2, 576, 128), bf16),
            vmem((2, 576, 1024), bf16),
            vmem((3584, 1024), bf16),
            vmem((3584, 1024), bf16),
            vmem((1024, 3584), bf16),
            vmem((16, W), f32),
            vmem((2, 256, 256), bf16),
            vmem((2, 16, 16, W), bf16),
            vmem((PIECES, 4, 32, W), bf16),
            vmem((2, 32, W), f32),
            vmem((576, 128), bf16),
            vmem((576, 128), bf16),
            vmem((128, LAT), bf16),
            vmem((128, LAT), bf16),
            vmem((2, PIECES, 32, W), bf16),
            vmem((PIECES, 32, W), bf16),
            vmem((16, 16, W), bf16),
            vmem((15, 16, W), bf16),
            dma((5,)),
            dma,
            dma,
            dma((2,)),
            dma((2,)),
            dma((2,)),
            dma,
            dma,
            dma((2,)),
            dma((2,)),
            dma((2,)),
            dma((2,)),
            dma((2,)),
            dma((2,)),
            dma,
            dma,
        ],
        compiler_params=pltpu.CompilerParams(
            collective_id=0, has_side_effects=True, vmem_limit_bytes=56 * 2**20
        ),
        cost_estimate=pl.CostEstimate(
            flops=2_000_000_000, bytes_accessed=25_000_000, transcendentals=400_000
        ),
    )(
        *[
            pltpu.with_memory_space_constraint(operand, pltpu.HBM)
            for operand in (
                jnp.swapaxes(queries, 1, 2),
                jnp.swapaxes(latent_cache, 1, 2),
                lengths,
                trade_slot,
                tokens,
                routing,
                gate_weights,
                w_gate,
                w_up,
                w_down,
            )
        ]
    )
    return pl.pallas_call(
        finish,
        out_shape=(pltpu.HBM((2, 128, LAT), bf16), pltpu.HBM((2, PIECES * W), bf16)),
        in_specs=[pl.BlockSpec(memory_space=pltpu.VMEM)] * 2,
        out_specs=(hbm_spec,) * 2,
        scratch_shapes=[vmem((2, PIECES * W), f32), vmem((2, PIECES * W), bf16), dma((2,))],
    )(
        pltpu.with_memory_space_constraint(attended, pltpu.VMEM),
        pltpu.with_memory_space_constraint(rows, pltpu.VMEM),
    )


def solution(mesh):
    in_specs = (
        P(("rep", "dev"), None, None),
        P(("rep", "dev"), None, None),
        P("rep"),
        P("rep"),
        P(("rep", "dev"), None),
        P(("rep", "dev"), None),
        P(("rep", "dev"), None),
        P("dev", None, None),
        P("dev", None, None),
        P("dev", None, None),
    )
    out_specs = (P(("rep", "dev"), None, None), P(("rep", "dev"), None))
    return jax.shard_map(local, mesh=mesh, in_specs=in_specs, out_specs=out_specs, check_vma=False)
```

```python
import functools

import jax
import jax.numpy as jnp
from jax import lax
from jax.experimental import pallas as pl
from jax.experimental.pallas import tpu as pltpu
from jax.sharding import PartitionSpec as P

LAT = 512
W = 512
CUTS = ((0, 4), (4, 7))
BATCHES = ((0, 16),)
PIECES = 7
SLOTS = 8
score_scale = 192.0 ** (-0.5)
MESH = pl.DeviceIdType.MESH
f32 = jnp.float32
bf16 = jnp.bfloat16


def send(src, dst, send_sem, recv_sem, to):
    return pltpu.make_async_remote_copy(
        src_ref=src,
        dst_ref=dst,
        send_sem=send_sem,
        recv_sem=recv_sem,
        device_id={"dev": to},
        device_id_type=MESH,
    )


def all_fifteen(blocks, sem):
    pltpu.make_async_copy(blocks, blocks, sem).wait()


def attend(q_t, k_t, live):
    scores = (
        lax.dot_general(q_t, k_t, (((0,), (0,)), ((), ())), preferred_element_type=f32)
        * score_scale
    )
    position = lax.broadcasted_iota(jnp.int32, scores.shape, 1)
    scores = jnp.where(position < live, scores, -jnp.inf)
    weights = jnp.exp(scores - jnp.max(scores, axis=1, keepdims=True))
    shares = (weights / jnp.sum(weights, axis=1, keepdims=True)).astype(bf16)
    return lax.dot_general(
        shares, k_t[:LAT], (((1,), (1,)), ((), ())), preferred_element_type=f32
    ).astype(bf16)


def kernel(
    q_hbm, k_hbm, len_hbm, trade_hbm, tok_hbm, rout_hbm, gw_hbm, wg_hbm, wu_hbm, wd_hbm,
    att, exp_ref,
    lengths, trade_slot, tok, rout, gw, q, k, wg, wu, wd, stage, perm, gathered, tok_rows, factors,
    q_out, q_in, o_out, o_in, sums, mate_in, back, landed,
    small_sem, q_sem, k_sem, wg_sem, wu_sem, wd_sem,
    tok_s, tok_r, fwd_s, fwd_r, trade_s, trade_r, mate_s, mate_r, back_s, back_r,
):
    me = lax.axis_index("dev")
    chip, core = lax.div(me, 2), lax.rem(me, 2)
    cx, cz = lax.div(chip, 4), lax.rem(chip, 4)
    other_core = 1 - core
    mate = chip * 2 + other_core
    partner = lax.rem(me + 16, 32)
    xs = [cx] + [lax.rem(cx + d, 4) for d in (1, 2, 3)]
    zs = [cz] + [lax.rem(cz + d, 4) for d in (1, 2, 3)]
    away = [(2, 2), (2, 1), (3, 2), (2, 3), (1, 2), (1, 1), (3, 3), (3, 1), (1, 3), (2, 0), (0, 2), (1, 0), (0, 3), (3, 0), (0, 1)]
    to = [(xs[dx] * 4 + zs[dz]) * 2 + core for dx, dz in away]
    source = [(xs[(4 - dx) % 4] * 4 + zs[(4 - dz) % 4]) * 2 + core for dx, dz in away]

    loads = [
        pltpu.make_async_copy(tok_hbm, tok, small_sem.at[0]),
        pltpu.make_async_copy(rout_hbm, rout, small_sem.at[1]),
        pltpu.make_async_copy(gw_hbm, gw, small_sem.at[2]),
        pltpu.make_async_copy(trade_hbm, trade_slot, small_sem.at[3]),
        pltpu.make_async_copy(len_hbm, lengths, small_sem.at[4]),
        pltpu.make_async_copy(q_hbm, q, q_sem),
        pltpu.make_async_copy(k_hbm, k, k_sem),
    ]
    tok_load, rout_load, gw_load, trade_load, len_load, q_load, k_load = loads
    wg_loads, wu_loads, wd_loads = [], [], []
    for i, (first, last) in enumerate(CUTS):
        rows = pl.ds(first * W, (last - first) * W)
        wg_loads.append(pltpu.make_async_copy(wg_hbm.at[0, rows], wg.at[rows], wg_sem.at[i]))
        wu_loads.append(pltpu.make_async_copy(wu_hbm.at[0, rows], wu.at[rows], wu_sem.at[i]))
        wd_loads.append(
            pltpu.make_async_copy(wd_hbm.at[0, :, rows], wd.at[:, rows], wd_sem.at[i])
        )
    for load in loads[:3]:
        load.start()
    barrier = pltpu.get_barrier_semaphore()
    for other in to + [mate]:
        pl.semaphore_signal(barrier, inc=1, device_id={"dev": other}, device_id_type=MESH)
    for load in loads[3:]:
        load.start()

    tok_load.wait()
    rout_load.wait()
    gw_load.wait()
    tokens = tok[...].astype(f32)
    lane = lax.broadcasted_iota(jnp.int32, (2, W), 1)
    factor = jnp.zeros((2, W), f32)
    for top in range(8):
        expert, weight = rout[:, top : top + 1], gw[:, top : top + 1]
        hit = (lane == expert) | (lane == expert + 32)
        factor = factor + jnp.where(hit, weight, 0.0)
    high = factor.astype(bf16).astype(f32)
    factor = jnp.where(lane < 32, high, factor - high)
    for t in range(2):
        for s in range(PIECES):
            stage[t * SLOTS + s : t * SLOTS + s + 1, :] = tokens[t : t + 1, s * W : (s + 1) * W]
        stage[t * SLOTS + PIECES : (t + 1) * SLOTS, :] = factor[t : t + 1]
    gathered[core, 15] = stage[...].astype(bf16)
    for i in range(2):
        wg_loads[i].start()
        wu_loads[i].start()

    pl.semaphore_wait(barrier, 16)

    own = gathered.at[core, 15]
    tok_copies = [
        send(own, gathered.at[core, i], tok_s, tok_r, to[i]) for i in range(15)
    ]
    for copy in tok_copies:
        copy.start()

    tok_rows[:, 2:] = jnp.zeros((PIECES, 2, 32, W), bf16)
    row = lax.broadcasted_iota(jnp.int32, (256, 256), 0)
    col = lax.broadcasted_iota(jnp.int32, (256, 256), 1)
    perm[0] = jnp.where(col == (row & 31) * SLOTS + (row >> 5), 1.0, 0.0).astype(bf16)
    perm[1] = jnp.where(row == (col & 31) * SLOTS + (col >> 5), 1.0, 0.0).astype(bf16)

    trade_load.wait()
    len_load.wait()
    trade_at = trade_slot[me % 16]
    keep_at = 1 - trade_at
    q_load.wait()
    q_out[...] = q[trade_at]
    q_copy = send(q_out, q_in, trade_s.at[0], trade_r.at[0], partner)
    q_copy.start()

    k_load.wait()
    kept = attend(q[keep_at], k[keep_at], lengths[me * 2 + keep_at])
    for i in range(2):
        wd_loads[i].start()

    def spread(side):
        rows = jnp.dot(
            perm[0], gathered[side].reshape(256, W), preferred_element_type=f32
        )
        for s in range(PIECES):
            tok_rows[s, side] = rows[s * 32 : (s + 1) * 32].astype(bf16)
        factors[side] = rows[PIECES * 32 :]

    fwd_copies = []
    for i, (first, last) in enumerate(BATCHES):
        all_fifteen(gathered.at[core, pl.ds(0, 15)], tok_r)
        batch = gathered.at[core, pl.ds(first, last - first)]
        fwd_copies.append(send(batch, batch, fwd_s.at[i], fwd_r.at[i], mate))
        fwd_copies[i].start()
    spread(core)
    for copy in fwd_copies:
        copy.wait_recv()
    spread(other_core)

    gate = jnp.zeros((128, 1024), f32)
    up = jnp.zeros((128, 1024), f32)
    for i, (first, last) in enumerate(CUTS):
        if i == 1:
            q_copy.wait_recv()
            o_out[...] = attend(q_in[...], k[trade_at], lengths[me * 2 + trade_at])
            o_copy = send(o_out, o_in, trade_s.at[1], trade_r.at[1], partner)
            o_copy.start()
        wg_loads[i].wait()
        wu_loads[i].wait()
        for s in range(first, last):
            x = tok_rows[s].reshape(128, W)
            rows = slice(s * W, (s + 1) * W)
            gate += jnp.dot(x, wg[rows, :], preferred_element_type=f32)
            up += jnp.dot(x, wu[rows, :], preferred_element_type=f32)
    gate, up = gate[:64], up[:64]
    hidden = (gate / (1.0 + jnp.exp(-gate)) * up).astype(bf16)
    hidden = jnp.concatenate([hidden, jnp.zeros((64, 1024), bf16)], axis=0)
    lane = lax.broadcasted_iota(jnp.int32, (64, W), 1)
    mine = (lane == me) | (lane == me + 32)
    weight = jnp.sum(jnp.where(mine, factors[...].reshape(64, W), 0.0), axis=1, keepdims=True)

    mate_copies = []
    for i, (first, last) in enumerate(CUTS):
        wd_loads[i].wait()
        for s in range(first, last):
            y = jnp.dot(hidden, wd[:, s * W : (s + 1) * W], preferred_element_type=f32)[:64]
            y = (y.astype(bf16).astype(f32) * weight).astype(bf16)
            sums[0, s] = y[:32]
            sums[1, s] = y[32:]
        cut = pl.ds(first, last - first)
        mate_copies.append(
            send(sums.at[other_core, cut], mate_in.at[cut], mate_s.at[i], mate_r.at[i], mate)
        )
        mate_copies[i].start()
    for copy in mate_copies:
        copy.wait_recv()
    part = (sums[core].astype(f32) + mate_in[...].astype(f32)).astype(bf16)
    part = jnp.concatenate([part.reshape(PIECES * 32, W), jnp.zeros((32, W), bf16)], axis=0)
    back[...] = (
        jnp.dot(perm[1], part, preferred_element_type=f32).astype(bf16).reshape(16, 16, W)
    )
    back_copies = [
        send(back.at[i], landed.at[i], back_s, back_r, source[i])
        for i in range(15)
    ]
    for copy in back_copies:
        copy.start()

    all_fifteen(gathered.at[core, pl.ds(0, 15)], tok_s)
    for copy in mate_copies + fwd_copies + [q_copy, o_copy]:
        copy.wait_send()
    o_copy.wait_recv()
    arrived = o_in[...]
    att[0] = jnp.where(trade_at == 0, arrived, kept)
    att[1] = jnp.where(trade_at == 1, arrived, kept)

    all_fifteen(landed, back_r)
    total = back[15].astype(f32)
    for i in range(15):
        total += landed[i].astype(f32)
    exp_ref[...] = total.astype(bf16)
    all_fifteen(landed, back_s)


def finish(att_ref, row_ref, att_hbm, exp_hbm, line, exp, sem):
    att_copy = pltpu.make_async_copy(att_ref, att_hbm, sem.at[0])
    att_copy.start()
    rows = row_ref[...].astype(f32)
    for t in range(2):
        for s in range(PIECES):
            line[t : t + 1, s * W : (s + 1) * W] = rows[t * SLOTS + s : t * SLOTS + s + 1]
    exp[...] = line[...].astype(bf16)
    exp_copy = pltpu.make_async_copy(exp, exp_hbm, sem.at[1])
    exp_copy.start()
    att_copy.wait()
    exp_copy.wait()


def local(
    queries, latent_cache, lengths, trade_slot, tokens, routing, gate_weights, w_gate, w_up, w_down
):
    hbm_spec = pl.BlockSpec(memory_space=pltpu.HBM)
    dma = pltpu.SemaphoreType.DMA
    vmem = pltpu.VMEM
    attended, rows = pl.pallas_call(
        kernel,
        out_shape=(
            pltpu.VMEM((2, 128, LAT), bf16),
            pltpu.VMEM((16, W), bf16),
        ),
        in_specs=[hbm_spec] * 10,
        out_specs=(pl.BlockSpec(memory_space=pltpu.VMEM),) * 2,
        scratch_shapes=[
            pltpu.SMEM((64,), jnp.int32),
            pltpu.SMEM((16,), jnp.int32),
            vmem((2, 3584), bf16),
            vmem((2, 8), jnp.int32),
            vmem((2, 8), f32),
            vmem((2, 576, 128), bf16),
            vmem((2, 576, 1024), bf16),
            vmem((3584, 1024), bf16),
            vmem((3584, 1024), bf16),
            vmem((1024, 3584), bf16),
            vmem((16, W), f32),
            vmem((2, 256, 256), bf16),
            vmem((2, 16, 16, W), bf16),
            vmem((PIECES, 4, 32, W), bf16),
            vmem((2, 32, W), f32),
            vmem((576, 128), bf16),
            vmem((576, 128), bf16),
            vmem((128, LAT), bf16),
            vmem((128, LAT), bf16),
            vmem((2, PIECES, 32, W), bf16),
            vmem((PIECES, 32, W), bf16),
            vmem((16, 16, W), bf16),
            vmem((15, 16, W), bf16),
            dma((5,)),
            dma,
            dma,
            dma((2,)),
            dma((2,)),
            dma((2,)),
            dma,
            dma,
            dma((2,)),
            dma((2,)),
            dma((2,)),
            dma((2,)),
            dma((2,)),
            dma((2,)),
            dma,
            dma,
        ],
        compiler_params=pltpu.CompilerParams(
            collective_id=0, has_side_effects=True, vmem_limit_bytes=56 * 2**20
        ),
        cost_estimate=pl.CostEstimate(
            flops=2_000_000_000, bytes_accessed=25_000_000, transcendentals=400_000
        ),
    )(
        *[
            pltpu.with_memory_space_constraint(operand, pltpu.HBM)
            for operand in (
                jnp.swapaxes(queries, 1, 2),
                jnp.swapaxes(latent_cache, 1, 2),
                lengths,
                trade_slot,
                tokens,
                routing,
                gate_weights,
                w_gate,
                w_up,
                w_down,
            )
        ]
    )
    return pl.pallas_call(
        finish,
        out_shape=(pltpu.HBM((2, 128, LAT), bf16), pltpu.HBM((2, PIECES * W), bf16)),
        in_specs=[pl.BlockSpec(memory_space=pltpu.VMEM)] * 2,
        out_specs=(hbm_spec,) * 2,
        scratch_shapes=[vmem((2, PIECES * W), f32), vmem((2, PIECES * W), bf16), dma((2,))],
    )(
        pltpu.with_memory_space_constraint(attended, pltpu.VMEM),
        pltpu.with_memory_space_constraint(rows, pltpu.VMEM),
    )


def solution(mesh):
    in_specs = (
        P(("rep", "dev"), None, None),
        P(("rep", "dev"), None, None),
        P("rep"),
        P("rep"),
        P(("rep", "dev"), None),
        P(("rep", "dev"), None),
        P(("rep", "dev"), None),
        P("dev", None, None),
        P("dev", None, None),
        P("dev", None, None),
    )
    out_specs = (P(("rep", "dev"), None, None), P(("rep", "dev"), None))
    return jax.shard_map(local, mesh=mesh, in_specs=in_specs, out_specs=out_specs, check_vma=False)
```

```python
import functools

import jax
import jax.numpy as jnp
from jax import lax
from jax.experimental import pallas as pl
from jax.experimental.pallas import tpu as pltpu
from jax.sharding import PartitionSpec as P

LAT = 512
W = 512
CUTS = ((0, 4), (4, 7))
BATCHES = ((0, 16),)
PIECES = 7
SLOTS = 8
score_scale = 192.0 ** (-0.5)
MESH = pl.DeviceIdType.MESH
f32 = jnp.float32
bf16 = jnp.bfloat16


def send(src, dst, send_sem, recv_sem, to):
    return pltpu.make_async_remote_copy(
        src_ref=src,
        dst_ref=dst,
        send_sem=send_sem,
        recv_sem=recv_sem,
        device_id={"dev": to},
        device_id_type=MESH,
    )


def all_fifteen(blocks, sem):
    pltpu.make_async_copy(blocks, blocks, sem).wait()


def attend(q_t, k_t, live):
    scores = (
        lax.dot_general(q_t, k_t, (((0,), (0,)), ((), ())), preferred_element_type=f32)
        * score_scale
    )
    position = lax.broadcasted_iota(jnp.int32, scores.shape, 1)
    scores = jnp.where(position < live, scores, -jnp.inf)
    weights = jnp.exp(scores - jnp.max(scores, axis=1, keepdims=True))
    shares = (weights / jnp.sum(weights, axis=1, keepdims=True)).astype(bf16)
    return lax.dot_general(
        shares, k_t[:LAT], (((1,), (1,)), ((), ())), preferred_element_type=f32
    ).astype(bf16)


def kernel(
    q_hbm, k_hbm, len_hbm, trade_hbm, tok_hbm, rout_hbm, gw_hbm, wg_hbm, wu_hbm, wd_hbm,
    att, exp_ref,
    lengths, trade_slot, tok, rout, gw, q, k, wg, wu, wd, stage, perm, gathered, tok_rows, factors,
    q_out, q_in, o_out, o_in, sums, mate_in, back, landed,
    small_sem, q_sem, k_sem, wg_sem, wu_sem, wd_sem,
    tok_s, tok_r, fwd_s, fwd_r, trade_s, trade_r, mate_s, mate_r, back_s, back_r,
):
    me = lax.axis_index("dev")
    chip, core = lax.div(me, 2), lax.rem(me, 2)
    cx, cz = lax.div(chip, 4), lax.rem(chip, 4)
    other_core = 1 - core
    mate = chip * 2 + other_core
    partner = lax.rem(me + 16, 32)
    xs = [cx] + [lax.rem(cx + d, 4) for d in (1, 2, 3)]
    zs = [cz] + [lax.rem(cz + d, 4) for d in (1, 2, 3)]
    away = [(2, 2), (2, 1), (3, 2), (2, 3), (1, 2), (1, 1), (3, 3), (3, 1), (1, 3), (2, 0), (0, 2), (1, 0), (0, 3), (3, 0), (0, 1)]
    to = [(xs[dx] * 4 + zs[dz]) * 2 + core for dx, dz in away]
    source = [(xs[(4 - dx) % 4] * 4 + zs[(4 - dz) % 4]) * 2 + core for dx, dz in away]

    loads = [
        pltpu.make_async_copy(tok_hbm, tok, small_sem.at[0]),
        pltpu.make_async_copy(rout_hbm, rout, small_sem.at[1]),
        pltpu.make_async_copy(gw_hbm, gw, small_sem.at[2]),
        pltpu.make_async_copy(trade_hbm, trade_slot, small_sem.at[3]),
        pltpu.make_async_copy(len_hbm, lengths, small_sem.at[4]),
        pltpu.make_async_copy(q_hbm, q, q_sem),
        pltpu.make_async_copy(k_hbm, k, k_sem),
    ]
    tok_load, rout_load, gw_load, trade_load, len_load, q_load, k_load = loads
    wg_loads, wu_loads, wd_loads = [], [], []
    for i, (first, last) in enumerate(CUTS):
        rows = pl.ds(first * W, (last - first) * W)
        wg_loads.append(pltpu.make_async_copy(wg_hbm.at[0, rows], wg.at[rows], wg_sem.at[i]))
        wu_loads.append(pltpu.make_async_copy(wu_hbm.at[0, rows], wu.at[rows], wu_sem.at[i]))
        wd_loads.append(
            pltpu.make_async_copy(wd_hbm.at[0, :, rows], wd.at[:, rows], wd_sem.at[i])
        )
    for load in loads[:3]:
        load.start()
    barrier = pltpu.get_barrier_semaphore()
    for other in to + [mate]:
        pl.semaphore_signal(barrier, inc=1, device_id={"dev": other}, device_id_type=MESH)
    for load in loads[3:]:
        load.start()

    tok_load.wait()
    rout_load.wait()
    gw_load.wait()
    tokens = tok[...].astype(f32)
    lane = lax.broadcasted_iota(jnp.int32, (2, W), 1)
    factor = jnp.zeros((2, W), f32)
    for top in range(8):
        expert, weight = rout[:, top : top + 1], gw[:, top : top + 1]
        hit = (lane == expert) | (lane == expert + 32)
        factor = factor + jnp.where(hit, weight, 0.0)
    high = factor.astype(bf16).astype(f32)
    factor = jnp.where(lane < 32, high, factor - high)
    for t in range(2):
        for s in range(PIECES):
            stage[t * SLOTS + s : t * SLOTS + s + 1, :] = tokens[t : t + 1, s * W : (s + 1) * W]
        stage[t * SLOTS + PIECES : (t + 1) * SLOTS, :] = factor[t : t + 1]
    gathered[core, 15] = stage[...].astype(bf16)
    for i in range(2):
        wg_loads[i].start()
        wu_loads[i].start()

    pl.semaphore_wait(barrier, 16)

    own = gathered.at[core, 15]
    tok_copies = [
        send(own, gathered.at[core, i], tok_s, tok_r, to[i]) for i in range(15)
    ]
    for copy in tok_copies:
        copy.start()

    tok_rows[:, 2:] = jnp.zeros((PIECES, 2, 32, W), bf16)
    row = lax.broadcasted_iota(jnp.int32, (256, 256), 0)
    col = lax.broadcasted_iota(jnp.int32, (256, 256), 1)
    perm[0] = jnp.where(col == (row & 31) * SLOTS + (row >> 5), 1.0, 0.0).astype(bf16)
    perm[1] = jnp.where(row == (col & 31) * SLOTS + (col >> 5), 1.0, 0.0).astype(bf16)

    trade_load.wait()
    len_load.wait()
    trade_at = trade_slot[me % 16]
    keep_at = 1 - trade_at
    q_load.wait()
    q_out[...] = q[trade_at]
    q_copy = send(q_out, q_in, trade_s.at[0], trade_r.at[0], partner)
    q_copy.start()

    k_load.wait()
    kept = attend(q[keep_at], k[keep_at], lengths[me * 2 + keep_at])
    for i in range(2):
        wd_loads[i].start()

    def spread(side):
        rows = jnp.dot(
            perm[0], gathered[side].reshape(256, W), preferred_element_type=f32
        )
        for s in range(PIECES):
            tok_rows[s, side] = rows[s * 32 : (s + 1) * 32].astype(bf16)
        factors[side] = rows[PIECES * 32 :]

    fwd_copies = []
    for i, (first, last) in enumerate(BATCHES):
        all_fifteen(gathered.at[core, pl.ds(0, 15)], tok_r)
        batch = gathered.at[core, pl.ds(first, last - first)]
        fwd_copies.append(send(batch, batch, fwd_s.at[i], fwd_r.at[i], mate))
        fwd_copies[i].start()
    spread(core)
    for copy in fwd_copies:
        copy.wait_recv()
    spread(other_core)

    gate = jnp.zeros((128, 1024), f32)
    up = jnp.zeros((128, 1024), f32)
    for i, (first, last) in enumerate(CUTS):
        if i == 1:
            q_copy.wait_recv()
            o_out[...] = attend(q_in[...], k[trade_at], lengths[me * 2 + trade_at])
            o_copy = send(o_out, o_in, trade_s.at[1], trade_r.at[1], partner)
            o_copy.start()
        wg_loads[i].wait()
        wu_loads[i].wait()
        for s in range(first, last):
            x = tok_rows[s].reshape(128, W)
            rows = slice(s * W, (s + 1) * W)
            gate += jnp.dot(x, wg[rows, :], preferred_element_type=f32)
            up += jnp.dot(x, wu[rows, :], preferred_element_type=f32)
    gate, up = gate[:64], up[:64]
    hidden = (gate / (1.0 + jnp.exp(-gate)) * up).astype(bf16)
    hidden = jnp.concatenate([hidden, jnp.zeros((64, 1024), bf16)], axis=0)
    lane = lax.broadcasted_iota(jnp.int32, (64, W), 1)
    mine = (lane == me) | (lane == me + 32)
    weight = jnp.sum(jnp.where(mine, factors[...].reshape(64, W), 0.0), axis=1, keepdims=True)

    mate_copies = []
    for i, (first, last) in enumerate(CUTS):
        wd_loads[i].wait()
        for s in range(first, last):
            y = jnp.dot(hidden, wd[:, s * W : (s + 1) * W], preferred_element_type=f32)[:64]
            y = (y.astype(bf16).astype(f32) * weight).astype(bf16)
            sums[0, s] = y[:32]
            sums[1, s] = y[32:]
        cut = pl.ds(first, last - first)
        mate_copies.append(
            send(sums.at[other_core, cut], mate_in.at[cut], mate_s.at[i], mate_r.at[i], mate)
        )
        mate_copies[i].start()
    blocks = jnp.zeros((256, W), f32)
    for i, (first, last) in enumerate(CUTS):
        mate_copies[i].wait_recv()
        cut = pl.ds(first, last - first)
        part = (sums[core, cut].astype(f32) + mate_in[cut].astype(f32)).astype(bf16)
        part = part.reshape((last - first) * 32, W)
        if last == PIECES:
            part = jnp.concatenate([part, jnp.zeros((32, W), bf16)], axis=0)
        blocks += jnp.dot(
            perm[1, :, first * 32 : first * 32 + 128], part, preferred_element_type=f32
        )
    back[...] = blocks.astype(bf16).reshape(16, 16, W)
    back_copies = [
        send(back.at[i], landed.at[i], back_s, back_r, source[i])
        for i in range(15)
    ]
    for copy in back_copies:
        copy.start()

    all_fifteen(gathered.at[core, pl.ds(0, 15)], tok_s)
    for copy in mate_copies + fwd_copies + [q_copy, o_copy]:
        copy.wait_send()
    o_copy.wait_recv()
    arrived = o_in[...]
    att[0] = jnp.where(trade_at == 0, arrived, kept)
    att[1] = jnp.where(trade_at == 1, arrived, kept)

    all_fifteen(landed, back_r)
    total = back[15].astype(f32)
    for i in range(15):
        total += landed[i].astype(f32)
    exp_ref[...] = total.astype(bf16)
    all_fifteen(landed, back_s)


def finish(att_ref, row_ref, att_hbm, exp_hbm, line, exp, sem):
    att_copy = pltpu.make_async_copy(att_ref, att_hbm, sem.at[0])
    att_copy.start()
    rows = row_ref[...].astype(f32)
    for t in range(2):
        for s in range(PIECES):
            line[t : t + 1, s * W : (s + 1) * W] = rows[t * SLOTS + s : t * SLOTS + s + 1]
    exp[...] = line[...].astype(bf16)
    exp_copy = pltpu.make_async_copy(exp, exp_hbm, sem.at[1])
    exp_copy.start()
    att_copy.wait()
    exp_copy.wait()


def local(
    queries, latent_cache, lengths, trade_slot, tokens, routing, gate_weights, w_gate, w_up, w_down
):
    hbm_spec = pl.BlockSpec(memory_space=pltpu.HBM)
    dma = pltpu.SemaphoreType.DMA
    vmem = pltpu.VMEM
    attended, rows = pl.pallas_call(
        kernel,
        out_shape=(
            pltpu.VMEM((2, 128, LAT), bf16),
            pltpu.VMEM((16, W), bf16),
        ),
        in_specs=[hbm_spec] * 10,
        out_specs=(pl.BlockSpec(memory_space=pltpu.VMEM),) * 2,
        scratch_shapes=[
            pltpu.SMEM((64,), jnp.int32),
            pltpu.SMEM((16,), jnp.int32),
            vmem((2, 3584), bf16),
            vmem((2, 8), jnp.int32),
            vmem((2, 8), f32),
            vmem((2, 576, 128), bf16),
            vmem((2, 576, 1024), bf16),
            vmem((3584, 1024), bf16),
            vmem((3584, 1024), bf16),
            vmem((1024, 3584), bf16),
            vmem((16, W), f32),
            vmem((2, 256, 256), bf16),
            vmem((2, 16, 16, W), bf16),
            vmem((PIECES, 4, 32, W), bf16),
            vmem((2, 32, W), f32),
            vmem((576, 128), bf16),
            vmem((576, 128), bf16),
            vmem((128, LAT), bf16),
            vmem((128, LAT), bf16),
            vmem((2, PIECES, 32, W), bf16),
            vmem((PIECES, 32, W), bf16),
            vmem((16, 16, W), bf16),
            vmem((15, 16, W), bf16),
            dma((5,)),
            dma,
            dma,
            dma((2,)),
            dma((2,)),
            dma((2,)),
            dma,
            dma,
            dma((2,)),
            dma((2,)),
            dma((2,)),
            dma((2,)),
            dma((2,)),
            dma((2,)),
            dma,
            dma,
        ],
        compiler_params=pltpu.CompilerParams(
            collective_id=0, has_side_effects=True, vmem_limit_bytes=56 * 2**20
        ),
        cost_estimate=pl.CostEstimate(
            flops=2_000_000_000, bytes_accessed=25_000_000, transcendentals=400_000
        ),
    )(
        *[
            pltpu.with_memory_space_constraint(operand, pltpu.HBM)
            for operand in (
                jnp.swapaxes(queries, 1, 2),
                jnp.swapaxes(latent_cache, 1, 2),
                lengths,
                trade_slot,
                tokens,
                routing,
                gate_weights,
                w_gate,
                w_up,
                w_down,
            )
        ]
    )
    return pl.pallas_call(
        finish,
        out_shape=(pltpu.HBM((2, 128, LAT), bf16), pltpu.HBM((2, PIECES * W), bf16)),
        in_specs=[pl.BlockSpec(memory_space=pltpu.VMEM)] * 2,
        out_specs=(hbm_spec,) * 2,
        scratch_shapes=[vmem((2, PIECES * W), f32), vmem((2, PIECES * W), bf16), dma((2,))],
    )(
        pltpu.with_memory_space_constraint(attended, pltpu.VMEM),
        pltpu.with_memory_space_constraint(rows, pltpu.VMEM),
    )


def solution(mesh):
    in_specs = (
        P(("rep", "dev"), None, None),
        P(("rep", "dev"), None, None),
        P("rep"),
        P("rep"),
        P(("rep", "dev"), None),
        P(("rep", "dev"), None),
        P(("rep", "dev"), None),
        P("dev", None, None),
        P("dev", None, None),
        P("dev", None, None),
    )
    out_specs = (P(("rep", "dev"), None, None), P(("rep", "dev"), None))
    return jax.shard_map(local, mesh=mesh, in_specs=in_specs, out_specs=out_specs, check_vma=False)
```
